256 devices in a mesh: row: 8 (over z), col: 32 (over y, x, core).
Axes of the slice: x: 4, y: 4, z: 8, core: 2. Of those that a mesh axis runs over, the one named last changes fastest.
Arguments:
- matrix: float32 [12288, 12288], P('row', 'col'), may hold values from -160 to 160, as said below
- pattern: int32 [32, 32], replicated, may hold values from 0 to 1, as said below
- row_order: int32 [32], replicated, may hold values from 0 to 31, as said below
- col_order: int32 [32], replicated, may hold values from 0 to 31, as said below
Outputs:
- factored: float32 [12288, 12288], P('row', 'col')
The draws below stay inside these ranges and needn't reach their ends.
Inputs may be any that keep to these rules, and one draw needn't show every extreme that they name: `row_order`: a permutation of 0 to 31. `col_order`: a permutation of 0 to 31. Symmetric with ones on the diagonal; pattern[1, 0] = 1; pattern[I, J] = 1 whenever pattern[I, 0] = pattern[J, 0] = 1, and whenever pattern[I, 1] = pattern[J, 1] = 1 with I, J >= 1. `matrix`: read in natural block order the window is symmetric, and its retained lower blocks make the pivot block of supernode 0, and that of supernode 1 after the first update, positive definite.
All inputs are finite; a program needn't handle non-finite values.
Results may differ from the reference program's by a relative error of at most 0.0003.
Values sent between devices are 32-bit elements; how exact they have to be, the bound alone decides.
A program may use at most 128 MiB of HBM per device.

```python
import math
import jax
import jax.numpy as jnp
from jax import lax

BLOCK = 384
WINDOW = 32


def layout(key):
    indices = jnp.arange(WINDOW, dtype=jnp.int32)
    row_order = jax.random.permutation(jax.random.fold_in(key, 11), WINDOW).astype(jnp.int32)
    col_order = jax.random.permutation(jax.random.fold_in(key, 12), WINDOW).astype(jnp.int32)
    first = jax.random.randint(jax.random.fold_in(key, 13), (WINDOW,), 0, 2).astype(jnp.int32)
    first = jnp.where(indices <= 1, 1, first)
    second = jnp.maximum(first, jax.random.randint(jax.random.fold_in(key, 14), (WINDOW,), 0, 2).astype(jnp.int32))
    second = jnp.where(indices == 0, 0, jnp.where(indices == 1, 1, second))
    extra = jax.random.randint(jax.random.fold_in(key, 15), (WINDOW, WINDOW), 0, 4) == 0
    trailing = (indices[:, None] >= 2) & (indices[None, :] >= 2) & (indices[:, None] > indices[None, :])
    extra = extra & trailing
    extra = extra | extra.T
    linked = first[:, None] * first[None, :] + second[:, None] * second[None, :] > 0
    pattern = (linked | extra | (indices[:, None] == indices[None, :])).astype(jnp.int32)
    return (row_order, col_order, pattern, first, second)


def pivot_factor(key):
    lower_part = jnp.tril(jnp.ones((BLOCK, BLOCK), jnp.float32), -1)
    diagonal = jax.random.uniform(jax.random.fold_in(key, 1), (BLOCK,), jnp.float32, 1.0, 2.0)
    spread = jax.random.truncated_normal(jax.random.fold_in(key, 2), -4.0, 4.0, (BLOCK, BLOCK), jnp.float32)
    return jnp.diag(diagonal) + spread * (0.5 / math.sqrt(BLOCK)) * lower_part


def draw_matrix(key, part):
    row_order, col_order, pattern, first, second = layout(key)
    indices = jnp.arange(WINDOW, dtype=jnp.int32)
    order = WINDOW * BLOCK
    first_rows = jnp.repeat(((first == 1) & (indices >= 1)).astype(jnp.float32), BLOCK)
    second_rows = jnp.repeat(((second == 1) & (indices >= 2)).astype(jnp.float32), BLOCK)
    first_factor = jax.random.truncated_normal(jax.random.fold_in(key, 21), -4.0, 4.0, (order, BLOCK), jnp.float32) * 0.25 * first_rows[:, None]
    first_factor = first_factor.at[0:BLOCK].set(pivot_factor(jax.random.fold_in(key, 22)))
    second_factor = jax.random.truncated_normal(jax.random.fold_in(key, 23), -4.0, 4.0, (order, BLOCK), jnp.float32) * 0.25 * second_rows[:, None]
    second_factor = second_factor.at[BLOCK:2 * BLOCK].set(pivot_factor(jax.random.fold_in(key, 24)))
    noise = jax.random.truncated_normal(jax.random.fold_in(key, 25), -4.0, 4.0, (order, order), jnp.float32)
    noise = (noise + noise.T) * 0.7071
    relevant = ((indices[:, None] <= 1) | (indices[None, :] <= 1)) & (pattern == 1)
    keep_noise = 1.0 - jnp.repeat(jnp.repeat(relevant.astype(jnp.float32), BLOCK, axis=0), BLOCK, axis=1)
    natural = jnp.dot(first_factor, first_factor.T, precision=lax.Precision.HIGHEST)
    natural = natural + jnp.dot(second_factor, second_factor.T, precision=lax.Precision.HIGHEST)
    natural = natural + noise * keep_noise
    tiles = natural.reshape(WINDOW, BLOCK, WINDOW, BLOCK)
    stored = jnp.take(jnp.take(tiles, row_order, axis=0), col_order, axis=2)
    return stored.reshape(order, order)


def draw_pattern(key, part):
    return layout(key)[2]


def draw_row_order(key, part):
    return layout(key)[0]


def draw_col_order(key, part):
    return layout(key)[1]


def setup_inputs(seed: int = 0) -> dict:
    seeds = jax.random.split(jax.random.key(seed), 5)
    matrix = draw_matrix(jax.random.fold_in(seeds[4], 71), 0)
    pattern = draw_pattern(jax.random.fold_in(seeds[4], 71), 0)
    row_order = draw_row_order(jax.random.fold_in(seeds[4], 71), 0)
    col_order = draw_col_order(jax.random.fold_in(seeds[4], 71), 0)
    return {"matrix": matrix, "pattern": pattern, "row_order": row_order, "col_order": col_order}


def positions(order):
    indices = jnp.arange(order.shape[0], dtype=jnp.int32)
    return jnp.sum(jnp.where(order[None, :] == indices[:, None], indices[None, :], 0), axis=1).astype(jnp.int32)

def expand(flags, tall, broad):
    return jnp.repeat(jnp.repeat(flags, tall, axis=0), broad, axis=1)

def reference(matrix, pattern, row_order, col_order):
    total = row_order.shape[0]
    row_place = positions(row_order)
    col_place = positions(col_order)
    tiles = matrix.reshape(total, BLOCK, total, BLOCK)
    natural = jnp.take(jnp.take(tiles, row_place, axis=0), col_place, axis=2)
    natural = natural.reshape(total * BLOCK, total * BLOCK)
    indices = jnp.arange(total, dtype=jnp.int32)
    lower = indices[:, None] >= indices[None, :]
    retain = expand((pattern == 1) & lower, BLOCK, BLOCK).astype(natural.dtype)
    lower_full = expand(lower, BLOCK, BLOCK).astype(natural.dtype)
    current = natural * retain
    identity = jnp.eye(BLOCK, dtype=natural.dtype)
    for supernode in range(2):
        low_edge = supernode * BLOCK
        pivot_values = current[low_edge:low_edge + BLOCK, low_edge:low_edge + BLOCK]
        factor = jnp.linalg.cholesky(pivot_values)
        inverse = jax.scipy.linalg.solve_triangular(factor, identity, lower=True)
        struct_rows = ((pattern[:, supernode] == 1) & (indices > supernode)).astype(natural.dtype)
        panel = current[:, low_edge:low_edge + BLOCK] * jnp.repeat(struct_rows, BLOCK)[:, None]
        scaled = jnp.dot(panel, inverse.T, precision=lax.Precision.HIGHEST)
        current = current - jnp.dot(scaled, scaled.T, precision=lax.Precision.HIGHEST) * lower_full
        center = jnp.repeat(indices == supernode, BLOCK)
        column = jnp.where(center[:, None], jnp.tile(factor, (total, 1)), scaled)
        current = current.at[:, low_edge:low_edge + BLOCK].set(column)
    current = current * retain
    tiles = current.reshape(total, BLOCK, total, BLOCK)
    stored = jnp.take(jnp.take(tiles, row_order, axis=0), col_order, axis=2)
    return stored.reshape(total * BLOCK, total * BLOCK)
```

```python
import jax
import jax.numpy as jnp
from jax import lax
from jax.experimental import pallas as pl
from jax.experimental.pallas import tpu as pltpu
from jax.sharding import PartitionSpec as P

BLOCK = 384
TILE = 128
CHUNK = BLOCK // 16
SHARE = BLOCK // 8
MESH = pl.DeviceIdType.MESH
EXACT = lax.Precision.HIGHEST
F32 = jnp.float32
BF16 = jnp.bfloat16
ROWS_COLS = ((1,), (0,))
COLS_COLS = ((0,), (0,))
ROWS_ROWS = ((1,), (1,))


def product(left, right, over):
    return lax.dot_general(
        left, right, (over, ((), ())), precision=EXACT, preferred_element_type=F32
    )


def split(value):
    high = value.astype(BF16)
    return high, (value - high.astype(F32)).astype(BF16)


def product3(left, right, over):
    def part(a, b):
        return lax.dot_general(a, b, (over, ((), ())), preferred_element_type=F32)

    return part(left[0], right[0]) + (part(left[0], right[1]) + part(left[1], right[0]))


def lane(value, k):
    return jnp.broadcast_to(value[:, k : k + 1], (8, TILE))


def sublane(value, k):
    return jnp.broadcast_to(value[k : k + 1, :], (8, TILE))


def tree(terms):
    while len(terms) > 1:
        terms = [terms[i] + terms[i + 1] for i in range(0, len(terms), 2)]
    return terms[0]


def factor_tile(rows):
    lanes = lax.broadcasted_iota(jnp.int32, (8, TILE), 1)
    subs = lax.broadcasted_iota(jnp.int32, (8, TILE), 0)
    at = [subs == j for j in range(8)]
    a = list(rows)
    e = [jnp.where(lanes == subs + 8 * q, 1.0, 0.0).astype(F32) for q in range(16)]
    upper, inverse = [], []
    for p in range(16):
        ap, ep = a[p], e[p]
        c = [lane(ap, 8 * p + j) for j in range(8)]
        fa, fe, pivots = ap, ep, c[0]
        for j in range(8):
            pivot = sublane(c[j], j)
            scale = 1.0 / pivot
            cj = jnp.where(at[j], -1.0, c[j])
            if j:
                fa = jnp.where(at[j], ap, fa)
                fe = jnp.where(at[j], ep, fe)
                pivots = jnp.where(at[j], pivot, pivots)

            def step(x):
                return jnp.where(at[j], 0.0, x) - cj * (sublane(x, j) * scale)

            for k in range(j + 1, 8):
                c[k] = step(c[k])
            ap, ep = step(ap), step(ep)
        root = lax.rsqrt(pivots)
        upper.append(jnp.where(lanes >= subs + 8 * p, fa * root, 0.0))
        inverse.append(fe * root)
        wa = [sublane(ap, j) for j in range(8)]
        we = [sublane(ep, j) for j in range(8)]
        for q in range(p + 1, 16):
            cq = [lane(a[q], 8 * p + j) for j in range(8)]
            a[q] = a[q] - tree([cq[j] * wa[j] for j in range(8)])
            e[q] = e[q] - tree([cq[j] * we[j] for j in range(8)])
    return upper, inverse


def find(order_ref, wanted):
    place = jnp.int32(0)
    for t in range(32):
        place = place + (order_ref[t] == wanted).astype(jnp.int32) * t
    return jnp.minimum(place, 31)


def flag(condition):
    return condition.astype(jnp.int32).astype(F32)


def remote(src, dst, send, recv, row, col):
    return pltpu.make_async_remote_copy(
        src_ref=src,
        dst_ref=dst,
        send_sem=send,
        recv_sem=recv,
        device_id=(row, col),
        device_id_type=MESH,
    )


def each(count, skip, do):
    def turn(k, carry):
        @pl.when(k != skip)
        def _():
            do(k)

        return carry

    lax.fori_loop(0, count, turn, 0)


def kernel(
    pattern,
    row_order,
    col_order,
    matrix,
    out,
    staged,
    second,
    got0,
    got1,
    got23,
    zsend01,
    zsend2,
    zgot01,
    zgot2,
    pivot,
    work,
    ework,
    upper,
    inverse,
    cross,
    panels_own,
    panels_sib,
    shares,
    turned,
    scaled,
    a2a_send,
    got0_sem,
    got1_sem,
    got23_sem,
    z01_send,
    z01_recv,
    z2_send,
    z2_recv,
    piv_send,
    piv_recv,
    sib_send,
    sib_recv,
    p1_send,
    p1_recv,
    p2y_send,
    p2y_recv,
    p2x_send,
    p2x_recv,
    p3_send,
    p3_recv,
    c1_send,
    c1_recv,
    c2_send,
    c2_recv,
):
    row = lax.axis_index("row")
    col = lax.axis_index("col")
    chip, core = col // 2, col % 2
    y, x = chip // 4, chip % 4
    sibling = chip * 2 + (1 - core)

    barrier = pltpu.get_barrier_semaphore()

    def greet_col(k):
        pl.semaphore_signal(barrier, inc=1, device_id=(row, k), device_id_type=MESH)

    def greet_row(k):
        pl.semaphore_signal(barrier, inc=1, device_id=(k, col), device_id_type=MESH)

    each(32, col, greet_col)
    each(8, row, greet_row)

    place0, place1 = find(row_order, 0), find(row_order, 1)
    z0, z1 = place0 // 4, place1 // 4
    local0, local1 = place0 % 4, place1 % 4
    u0, u1 = find(col_order, 0), find(col_order, 1)
    same = (local0 == local1).astype(jnp.int32)
    step = (local1 - local0 + 4) % 4 + same
    order = [
        local0,
        (local0 + step) % 4,
        (local0 + 1 + (step == 1).astype(jnp.int32)) % 4,
        (local0 + 3 - (step == 3).astype(jnp.int32)) % 4,
    ]

    def stage(slot):
        staged[slot] = matrix[order[slot]]

    stage(0)
    pl.semaphore_wait(barrier, 31 + 7)

    def a2a(slot, got, got_sem, sends):
        def piece(k):
            return staged.at[slot, pl.ds(pl.multiple_of(k * CHUNK, 8), CHUNK)]

        def send(k):
            remote(
                piece(k), got.at[col], a2a_send.at[sends, k], got_sem.at[col], row, 2 * k
            ).start()

        each(16, jnp.where(core == 0, chip, 16), send)

        @pl.when(core == 0)
        def _():
            got[col] = staged[slot, pl.ds(pl.multiple_of(chip * CHUNK, 8), CHUNK), :]

    def a2a_wait(got, got_sem):
        def wait(k):
            remote(
                got.at[k], got.at[k], a2a_send.at[0, 0], got_sem.at[k], row, k
            ).wait_recv()

        each(32, col, wait)

    def a2a_sent(slot, sends):
        def wait(k):
            piece = staged.at[slot, pl.ds(pl.multiple_of(k * CHUNK, 8), CHUNK)]
            remote(
                piece, got0.at[col], a2a_send.at[sends, k], got0_sem.at[col], row, 2 * k
            ).wait_send()

        each(16, jnp.where(core == 0, chip, 16), wait)

    def piece23(k):
        return staged.at[pl.ds(2, 2), pl.ds(pl.multiple_of(k * CHUNK, 8), CHUNK)]

    def a2a23():
        def send(k):
            remote(
                piece23(k),
                got23.at[col],
                a2a_send.at[2, k],
                got23_sem.at[col],
                row,
                2 * k + 1,
            ).start()

        each(16, jnp.where(core == 1, chip, 16), send)

        @pl.when(core == 1)
        def _():
            got23[col] = staged[
                pl.ds(2, 2), pl.ds(pl.multiple_of(chip * CHUNK, 8), CHUNK), :
            ]

    def a2a23_sent():
        def wait(k):
            remote(
                piece23(k),
                got23.at[col],
                a2a_send.at[2, k],
                got23_sem.at[col],
                row,
                2 * k + 1,
            ).wait_send()

        each(16, jnp.where(core == 1, chip, 16), wait)

    def z_copy(src, got, send_sem, recv_sem, k):
        return remote(src, got.at[row], send_sem.at[k], recv_sem.at[row], k, col)

    def z_start(src, got, send_sem, recv_sem):
        each(8, row, lambda k: z_copy(src, got, send_sem, recv_sem, k).start())
        got[row] = src[...]

    def z_wait(src, got, send_sem, recv_sem):
        def wait(k):
            remote(
                src, got.at[k], send_sem.at[k], recv_sem.at[k], k, col
            ).wait_recv()

        each(8, row, wait)

    def z_sent(src, got, send_sem, recv_sem):
        each(8, row, lambda k: z_copy(src, got, send_sem, recv_sem, k).wait_send())

    def chunk_of(block, k):
        return pivot.at[block, pl.ds(pl.multiple_of(k * CHUNK, 8), CHUNK)]

    def piv_start(block):
        def send(k):
            remote(
                chunk_of(block, chip),
                chunk_of(block, chip),
                piv_send.at[block, k],
                piv_recv.at[block, chip],
                row,
                2 * k,
            ).start()

        each(16, chip, send)

    def piv_wait(block):
        def wait(k):
            remote(
                chunk_of(block, chip),
                chunk_of(block, k),
                piv_send.at[block, k],
                piv_recv.at[block, k],
                row,
                2 * k,
            ).wait_recv()

        each(16, chip, wait)

    def piv_sent(block):
        def wait(k):
            remote(
                chunk_of(block, chip),
                chunk_of(block, chip),
                piv_send.at[block, k],
                piv_recv.at[block, chip],
                row,
                2 * k,
            ).wait_send()

        each(16, chip, wait)

    def sib_copy(block):
        return remote(
            pivot.at[block],
            pivot.at[block],
            sib_send.at[block],
            sib_recv.at[block],
            row,
            sibling,
        )

    mine = pl.ds(pl.multiple_of(chip * CHUNK, 8), CHUNK)

    def panels_fill():
        @pl.when(core == 0)
        def _():
            for i, u in enumerate((u0, u1)):
                panels_own[i, 0, mine, :] = got0[u]
                panels_own[i, 1, mine, :] = got1[u]

        @pl.when(core == 1)
        def _():
            for i, u in enumerate((u0, u1)):
                panels_own[i, :, mine, :] = got23[u]

    def col_of(yy, xx):
        return (yy * 4 + xx) * 2 + core

    def p1_copy(i, k, at):
        there = col_of(y, k) if i == 0 else col_of(k, x)
        source = pl.ds(pl.multiple_of(at * CHUNK, 8), CHUNK)
        here = x if i == 0 else y
        return remote(
            panels_own.at[i, :, mine],
            panels_own.at[i, :, source],
            p1_send.at[i, k],
            p1_recv.at[i, here],
            row,
            there,
        )

    def p1_start():
        each(4, x, lambda k: p1_copy(0, k, chip).start())
        each(4, y, lambda k: p1_copy(1, k, chip).start())

    def p1_wait():
        def wait(i, k):
            at = y * 4 + k if i == 0 else k * 4 + x
            there = col_of(y, k) if i == 0 else col_of(k, x)
            source = pl.ds(pl.multiple_of(at * CHUNK, 8), CHUNK)
            remote(
                panels_own.at[i, :, mine],
                panels_own.at[i, :, source],
                p1_send.at[i, k],
                p1_recv.at[i, k],
                row,
                there,
            ).wait_recv()

        each(4, x, lambda k: wait(0, k))
        each(4, y, lambda k: wait(1, k))

    def p1_sent():
        each(4, x, lambda k: p1_copy(0, k, chip).wait_send())
        each(4, y, lambda k: p1_copy(1, k, chip).wait_send())

    def band(at):
        return panels_own.at[0, :, pl.ds(pl.multiple_of(at * 4 * CHUNK, 8), 4 * CHUNK)]

    def strip(yy, xx):
        return panels_own.at[
            1, :, pl.ds(pl.multiple_of((yy * 4 + xx) * CHUNK, 8), CHUNK)
        ]

    def p2_start():
        each(
            4,
            y,
            lambda k: remote(
                band(y), band(y), p2y_send.at[k], p2y_recv.at[y], row, col_of(k, x)
            ).start(),
        )

        def send(k):
            for yy in range(4):
                remote(
                    strip(yy, x),
                    strip(yy, x),
                    p2x_send.at[k, yy],
                    p2x_recv.at[x, yy],
                    row,
                    col_of(y, k),
                ).start()

        each(4, x, send)

    def p2_wait():
        each(
            4,
            y,
            lambda k: remote(
                band(y), band(k), p2y_send.at[k], p2y_recv.at[k], row, col_of(k, x)
            ).wait_recv(),
        )

        def wait(k):
            for yy in range(4):
                remote(
                    strip(yy, x),
                    strip(yy, k),
                    p2x_send.at[k, yy],
                    p2x_recv.at[k, yy],
                    row,
                    col_of(y, k),
                ).wait_recv()

        each(4, x, wait)

    def p2_sent():
        each(
            4,
            y,
            lambda k: remote(
                band(y), band(y), p2y_send.at[k], p2y_recv.at[y], row, col_of(k, x)
            ).wait_send(),
        )

        def wait(k):
            for yy in range(4):
                remote(
                    strip(yy, x),
                    strip(yy, x),
                    p2x_send.at[k, yy],
                    p2x_recv.at[x, yy],
                    row,
                    col_of(y, k),
                ).wait_send()

        each(4, x, wait)

    def p3_copy():
        return remote(panels_own, panels_sib, p3_send, p3_recv, row, sibling)

    def share(ref, i, k):
        return ref.at[i, pl.ds(pl.multiple_of(k * SHARE, 8), SHARE)]

    def c1_copy(i, k):
        src = staged.at[0] if i == 0 else second
        return remote(
            src.at[pl.ds(pl.multiple_of(k * SHARE, 8), SHARE)],
            shares.at[i, row],
            c1_send.at[i, k],
            c1_recv.at[i, row],
            k,
            col,
        )

    here = pl.ds(pl.multiple_of(row * SHARE, 8), SHARE)

    def c1_start():
        for i in range(2):
            each(8, row, lambda k: c1_copy(i, k).start())
        shares[0, row] = staged[0, here, :]
        shares[1, row] = second[here, :]

    def c1_wait():
        for i in range(2):
            each(
                8,
                row,
                lambda k: remote(
                    second.at[pl.ds(0, SHARE)],
                    shares.at[i, k],
                    c1_send.at[i, k],
                    c1_recv.at[i, k],
                    k,
                    col,
                ).wait_recv(),
            )

    def c1_sent():
        for i in range(2):
            each(8, row, lambda k: c1_copy(i, k).wait_send())

    def c2_copy(k, at):
        block = turned.at[:, pl.ds(pl.multiple_of(at * SHARE, 8), SHARE)]
        mine_ = turned.at[:, here]
        return mine_, block, k

    def c2_start():
        turned[0, here, :] = shares[0, z0]
        turned[1, here, :] = shares[1, z1]
        each(
            8,
            row,
            lambda k: remote(
                turned.at[:, here],
                turned.at[:, here],
                c2_send.at[k],
                c2_recv.at[row],
                k,
                col,
            ).start(),
        )

    def c2_wait():
        each(
            8,
            row,
            lambda k: remote(
                turned.at[:, here],
                turned.at[:, pl.ds(pl.multiple_of(k * SHARE, 8), SHARE)],
                c2_send.at[k],
                c2_recv.at[k],
                k,
                col,
            ).wait_recv(),
        )

    def c2_sent():
        each(
            8,
            row,
            lambda k: remote(
                turned.at[:, here],
                turned.at[:, here],
                c2_send.at[k],
                c2_recv.at[row],
                k,
                col,
            ).wait_send(),
        )

    a2a(0, got0, got0_sem, 0)
    stage(1)
    stage(2)
    stage(3)
    second[...] = staged[1 - same]
    upper[...] = jnp.zeros_like(upper)
    inverse[...] = jnp.zeros_like(inverse)
    ework[...] = jnp.zeros_like(ework)

    @pl.when(core == 0)
    def _():
        a2a_wait(got0, got0_sem)
        zsend01[0] = got0[u0]
        zsend01[1] = got0[u1]
        z_start(zsend01, zgot01, z01_send, z01_recv)
        z_wait(zsend01, zgot01, z01_send, z01_recv)
        pivot[0, mine, :] = zgot01[z0, 0]
        pivot[1, mine, :] = zgot01[z0, 1]
        piv_start(0)
        piv_start(1)
        piv_wait(0)
        sib_copy(0).start()

    @pl.when(core == 1)
    def _():
        sib_copy(0).wait_recv()

    a2a(1, got1, got1_sem, 1)
    c1_start()

    work[0] = pivot[0]

    def comm(b):
        @pl.when(b == 1)
        def _():
            @pl.when(core == 0)
            def _():
                piv_wait(1)
                sib_copy(1).start()
                a2a_wait(got1, got1_sem)
                weight = same.astype(F32)
                zsend2[...] = got0[u1] * weight + got1[u1] * (1.0 - weight)
                z_start(zsend2, zgot2, z2_send, z2_recv)

            a2a23()

        @pl.when(b == 2)
        def _():
            @pl.when(core == 0)
            def _():
                z_wait(zsend2, zgot2, z2_send, z2_recv)
                pivot[2, mine, :] = zgot2[z1]
                piv_start(2)

        @pl.when(b == 3)
        def _():
            @pl.when(core == 0)
            def _():
                piv_wait(2)
                sib_copy(2).start()

            @pl.when(core == 1)
            def _():
                a2a_wait(got23, got23_sem)

            panels_fill()
            p1_start()

            @pl.when(core == 1)
            def _():
                sib_copy(1).wait_recv()
                sib_copy(2).wait_recv()

            cross[...] = product(inverse[0], pivot[1], ROWS_COLS)
            work[1] = pivot[2] - product(cross[...], cross[...], COLS_COLS)

        @pl.when(b == 4)
        def _():
            p1_wait()
            p2_start()
            c1_wait()
            c2_start()

    def block_step(b, carry):
        comm(b)
        s = b // 3
        part = b % 3
        r0 = pl.multiple_of(part * TILE, TILE)
        tile = pl.ds(r0, TILE)
        rows = [
            work[s, pl.ds(pl.multiple_of(r0 + 8 * q, 8), 8), tile] for q in range(16)
        ]
        up, inv = factor_tile(rows)
        for q in range(16):
            at = pl.ds(pl.multiple_of(r0 + 8 * q, 8), 8)
            upper[s, at, tile] = up[q]
            inverse[s, at, tile] = inv[q]
        small = inverse[s, tile, tile]
        lanes = lax.broadcasted_iota(jnp.int32, (TILE, BLOCK), 1)
        after = lanes >= r0 + TILE
        before = lanes < r0
        down = jnp.where(after, product(small, work[s, tile, :], ROWS_COLS), 0.0)
        left = jnp.where(before, product(small, ework[s, tile, :], ROWS_COLS), 0.0)
        upper[s, tile, :] += down
        inverse[s, tile, :] += left

        @pl.when(part < 2)
        def _():
            work[s] -= product(down, down, COLS_COLS)
            ework[s] -= product(down, inverse[s, tile, :], COLS_COLS)

        return carry

    lax.fori_loop(0, 6, block_step, 0)

    j = col_order[col]
    mask0 = flag((pattern[j, 0] == 1) & (j > 0))
    mask1 = flag((pattern[j, 1] == 1) & (j > 1))
    is0, is1 = flag(j == 0), flag(j == 1)
    rest_of = flag(j > 1)
    c2_wait()
    v0 = split(inverse[0])
    v1 = split(inverse[1])
    cr = split(cross[...])
    r0 = product3(v0, split(turned[0] * mask0), ROWS_COLS)
    r0s = split(r0)
    r1 = product3(
        v1, split((turned[1] - product3(cr, r0s, COLS_COLS)) * mask1), ROWS_COLS
    )
    r1s = split(r1)
    p2_wait()
    p3_copy().start()

    place = [jnp.int32(0)] * 4
    for slot in range(4):
        for b in range(4):
            place[b] = place[b] + (order[slot] == b).astype(jnp.int32) * slot

    def update(half, ref):
        for k in range(2):
            first = 1 - half
            i = row_order[row * 4 + first * order[k] + half * order[2 + k]]
            m0 = flag((pattern[i, 0] == 1) & (i > 0))
            m1 = flag((pattern[i, 1] == 1) & (i > 1))
            s0 = product3(split(ref[0, k] * m0), v0, ROWS_ROWS)
            s0s = split(s0)
            rest = (ref[1, k] - product3(s0s, cr, ROWS_COLS)) * m1
            s1 = product3(split(rest), v1, ROWS_ROWS)
            change = product3(s0s, r0s, ROWS_COLS) + product3(
                split(s1), r1s, ROWS_COLS
            )
            scaled[half * 2 + k] = is0 * s0 + is1 * s1 - rest_of * change

    update(core, panels_own)
    p3_copy().wait_recv()
    update(1 - core, panels_sib)

    factors = [upper[s].T * flag(j == s) for s in range(2)]
    for b in range(4):
        i = row_order[row * 4 + b]
        keep = flag((pattern[i, j] == 1) & (i >= j))
        center0, center1 = flag((i == 0) & (j == 0)), flag((i == 1) & (j == 1))
        value = matrix[b] * rest_of + scaled[place[b]]
        out[b] = value * keep + factors[0] * center0 + factors[1] * center1

    a2a_sent(0, 0)
    a2a_sent(1, 1)
    a2a23_sent()
    p1_sent()
    p2_sent()
    p3_copy().wait_send()
    c1_sent()
    c2_sent()

    @pl.when(core == 0)
    def _():
        z_sent(zsend01, zgot01, z01_send, z01_recv)
        z_sent(zsend2, zgot2, z2_send, z2_recv)
        for block in range(3):
            piv_sent(block)
            sib_copy(block).wait_send()


def body(matrix, pattern, row_order, col_order):
    block = (BLOCK, BLOCK)
    vmem = lambda *shape: pltpu.VMEM(shape, F32)
    dma = lambda *shape: pltpu.SemaphoreType.DMA(shape)
    return pl.pallas_call(
        kernel,
        out_shape=jax.ShapeDtypeStruct((4, *block), F32),
        in_specs=[pl.BlockSpec(memory_space=pltpu.SMEM)] * 3
        + [pl.BlockSpec(memory_space=pltpu.VMEM)],
        out_specs=pl.BlockSpec(memory_space=pltpu.VMEM),
        scratch_shapes=[
            vmem(4, *block),
            vmem(*block),
            vmem(32, CHUNK, BLOCK),
            vmem(32, CHUNK, BLOCK),
            vmem(32, 2, CHUNK, BLOCK),
            vmem(2, CHUNK, BLOCK),
            vmem(CHUNK, BLOCK),
            vmem(8, 2, CHUNK, BLOCK),
            vmem(8, CHUNK, BLOCK),
            vmem(3, *block),
            vmem(2, *block),
            vmem(2, *block),
            vmem(2, *block),
            vmem(2, *block),
            vmem(*block),
            vmem(2, 2, *block),
            vmem(2, 2, *block),
            vmem(2, 8, SHARE, BLOCK),
            vmem(2, *block),
            vmem(4, *block),
            dma(3, 16),
            dma(32),
            dma(32),
            dma(32),
            dma(8),
            dma(8),
            dma(8),
            dma(8),
            dma(3, 16),
            dma(3, 16),
            dma(3),
            dma(3),
            dma(2, 4),
            dma(2, 4),
            dma(4),
            dma(4),
            dma(4, 4),
            dma(4, 4),
            pltpu.SemaphoreType.DMA,
            pltpu.SemaphoreType.DMA,
            dma(2, 8),
            dma(2, 8),
            dma(8),
            dma(8),
        ],
        compiler_params=pltpu.CompilerParams(
            collective_id=0, has_side_effects=True, vmem_limit_bytes=60 * 2**20
        ),
    )(pattern, row_order, col_order, matrix.reshape(4, *block)).reshape(matrix.shape)


def solution(mesh):
    in_specs = (P("row", "col"), P(), P(), P())
    out_specs = P("row", "col")
    return jax.shard_map(body, mesh=mesh, in_specs=in_specs, out_specs=out_specs, check_vma=False)
```

```python
import jax
import jax.numpy as jnp
from jax import lax
from jax.experimental import pallas as pl
from jax.experimental.pallas import tpu as pltpu
from jax.sharding import PartitionSpec as P

BLOCK = 384
TILE = 128
CHUNK = BLOCK // 16
SHARE = BLOCK // 8
MESH = pl.DeviceIdType.MESH
EXACT = lax.Precision.HIGHEST
F32 = jnp.float32
BF16 = jnp.bfloat16
ROWS_COLS = ((1,), (0,))
COLS_COLS = ((0,), (0,))
ROWS_ROWS = ((1,), (1,))


def product(left, right, over):
    return lax.dot_general(
        left, right, (over, ((), ())), precision=EXACT, preferred_element_type=F32
    )


def split(value):
    high = value.astype(BF16)
    return high, (value - high.astype(F32)).astype(BF16)


def product3(left, right, over):
    def part(a, b):
        return lax.dot_general(a, b, (over, ((), ())), preferred_element_type=F32)

    return part(left[0], right[0]) + (part(left[0], right[1]) + part(left[1], right[0]))


def lane(value, k):
    return jnp.broadcast_to(value[:, k : k + 1], (8, TILE))


def sublane(value, k):
    return jnp.broadcast_to(value[k : k + 1, :], (8, TILE))


def tree(terms):
    while len(terms) > 1:
        terms = [terms[i] + terms[i + 1] for i in range(0, len(terms), 2)]
    return terms[0]


def factor_tile(rows):
    lanes = lax.broadcasted_iota(jnp.int32, (8, TILE), 1)
    subs = lax.broadcasted_iota(jnp.int32, (8, TILE), 0)
    at = [subs == j for j in range(8)]
    a = list(rows)
    e = [jnp.where(lanes == subs + 8 * q, 1.0, 0.0).astype(F32) for q in range(16)]
    upper, inverse = [], []
    for p in range(16):
        ap, ep = a[p], e[p]
        c = [lane(ap, 8 * p + j) for j in range(8)]
        fa, fe, pivots = ap, ep, c[0]
        for j in range(8):
            pivot = sublane(c[j], j)
            scale = 1.0 / pivot
            cj = jnp.where(at[j], -1.0, c[j])
            if j:
                fa = jnp.where(at[j], ap, fa)
                fe = jnp.where(at[j], ep, fe)
                pivots = jnp.where(at[j], pivot, pivots)

            def step(x):
                return jnp.where(at[j], 0.0, x) - cj * (sublane(x, j) * scale)

            for k in range(j + 1, 8):
                c[k] = step(c[k])
            ap, ep = step(ap), step(ep)
        root = lax.rsqrt(pivots)
        upper.append(jnp.where(lanes >= subs + 8 * p, fa * root, 0.0))
        inverse.append(fe * root)
        wa = [sublane(ap, j) for j in range(8)]
        we = [sublane(ep, j) for j in range(8)]
        for q in range(p + 1, 16):
            cq = [lane(a[q], 8 * p + j) for j in range(8)]
            a[q] = a[q] - tree([cq[j] * wa[j] for j in range(8)])
            e[q] = e[q] - tree([cq[j] * we[j] for j in range(8)])
    return upper, inverse


def find(order_ref, wanted):
    place = jnp.int32(0)
    for t in range(32):
        place = place + (order_ref[t] == wanted).astype(jnp.int32) * t
    return jnp.minimum(place, 31)


def flag(condition):
    return condition.astype(jnp.int32).astype(F32)


def remote(src, dst, send, recv, row, col):
    return pltpu.make_async_remote_copy(
        src_ref=src,
        dst_ref=dst,
        send_sem=send,
        recv_sem=recv,
        device_id=(row, col),
        device_id_type=MESH,
    )


def each(count, me, do):
    for i in range(1, count):
        do((me + i) % count)


def kernel(
    pattern,
    row_order,
    col_order,
    matrix,
    out,
    staged,
    second,
    got0,
    got1,
    got23,
    zsend0,
    zsend1,
    zsend2,
    zgot0,
    zgot1,
    zgot2,
    pivot,
    work,
    ework,
    upper,
    inverse,
    cross,
    panels_own,
    panels_sib,
    shares,
    turned,
    scaled,
    a2a_send,
    got0_sem,
    got1_sem,
    got23_sem,
    z0_send,
    z0_recv,
    z1_send,
    z1_recv,
    z2_send,
    z2_recv,
    piv_send,
    piv_recv,
    sib_send,
    sib_recv,
    p1_send,
    p1_recv,
    p2_send,
    p2_recv,
    p3_send,
    p3_recv,
    c1_send,
    c1_recv,
    c2_send,
    c2_recv,
):
    row = lax.axis_index("row")
    col = lax.axis_index("col")
    chip, core = col // 2, col % 2
    y, x = chip // 4, chip % 4
    sibling = chip * 2 + (1 - core)

    barrier = pltpu.get_barrier_semaphore()

    def greet_col(k):
        pl.semaphore_signal(barrier, inc=1, device_id=(row, k), device_id_type=MESH)

    def greet_row(k):
        pl.semaphore_signal(barrier, inc=1, device_id=(k, col), device_id_type=MESH)

    each(32, col, greet_col)
    each(8, row, greet_row)

    place0, place1 = find(row_order, 0), find(row_order, 1)
    z0, z1 = place0 // 4, place1 // 4
    local0, local1 = place0 % 4, place1 % 4
    u0, u1 = find(col_order, 0), find(col_order, 1)
    same = (local0 == local1).astype(jnp.int32)
    step = (local1 - local0 + 4) % 4 + same
    order = [
        local0,
        (local0 + step) % 4,
        (local0 + 1 + (step == 1).astype(jnp.int32)) % 4,
        (local0 + 3 - (step == 3).astype(jnp.int32)) % 4,
    ]

    def stage(slot):
        staged[slot] = matrix[order[slot]]

    stage(0)
    pl.semaphore_wait(barrier, 31 + 7)

    def some(ref, count):
        return ref.at[pl.ds(0, count)]

    def arrived(ref, recv):
        remote(ref, ref, p3_send, recv, row, sibling).wait_recv()

    def left(ref, send):
        remote(ref, ref, send, p3_recv, row, sibling).wait_send()

    def a2a(slot, got, got_sem, sends):
        def piece(k):
            return staged.at[slot, pl.ds(pl.multiple_of(k * CHUNK, 8), CHUNK)]

        def send(k):
            remote(
                piece(k), got.at[col], a2a_send.at[sends], got_sem, row, 2 * k
            ).start()

        each(16, chip, send)

        @pl.when(core == 1)
        def _():
            send(chip)

        @pl.when(core == 0)
        def _():
            got[col] = staged[slot, pl.ds(pl.multiple_of(chip * CHUNK, 8), CHUNK), :]

    def a2a_wait(got, got_sem):
        arrived(some(got, 31), got_sem)

    def a2a_sent(sends):
        @pl.when(core == 0)
        def _():
            left(some(got0, 15), a2a_send.at[sends])

        @pl.when(core == 1)
        def _():
            left(some(got0, 16), a2a_send.at[sends])

    def piece23(k):
        return staged.at[pl.ds(2, 2), pl.ds(pl.multiple_of(k * CHUNK, 8), CHUNK)]

    def a2a23():
        def send(k):
            remote(
                piece23(k),
                got23.at[col],
                a2a_send.at[2],
                got23_sem,
                row,
                2 * k + 1,
            ).start()

        each(16, chip, send)

        @pl.when(core == 0)
        def _():
            send(chip)

        @pl.when(core == 1)
        def _():
            got23[col] = staged[
                pl.ds(2, 2), pl.ds(pl.multiple_of(chip * CHUNK, 8), CHUNK), :
            ]

    def a2a23_sent():
        @pl.when(core == 0)
        def _():
            left(some(got23, 16), a2a_send.at[2])

        @pl.when(core == 1)
        def _():
            left(some(got23, 15), a2a_send.at[2])

    def z_start(src, got, send_sem, recv_sem):
        each(
            8,
            row,
            lambda k: remote(src, got.at[row], send_sem, recv_sem, k, col).start(),
        )
        got[row] = src[...]

    def z_wait(src, got, send_sem, recv_sem):
        arrived(some(got, 7), recv_sem)

    def z_sent(src, got, send_sem, recv_sem):
        left(some(got, 7), send_sem)

    def chunk_of(block, k):
        return pivot.at[block, pl.ds(pl.multiple_of(k * CHUNK, 8), CHUNK)]

    def piv_start(block):
        def send(k):
            remote(
                chunk_of(block, chip),
                chunk_of(block, chip),
                piv_send.at[block],
                piv_recv.at[block],
                row,
                2 * k,
            ).start()

        each(16, chip, send)

    def piv_wait(block):
        arrived(pivot.at[block, pl.ds(0, 15 * CHUNK)], piv_recv.at[block])

    def piv_sent(block):
        left(pivot.at[block, pl.ds(0, 15 * CHUNK)], piv_send.at[block])

    def sib_copy(block):
        return remote(
            pivot.at[block],
            pivot.at[block],
            sib_send.at[block],
            sib_recv.at[block],
            row,
            sibling,
        )

    mine = pl.ds(pl.multiple_of(chip * CHUNK, 8), CHUNK)

    def panels_fill():
        @pl.when(core == 0)
        def _():
            for i, u in enumerate((u0, u1)):
                panels_own[i, 0, mine, :] = got0[u]
                panels_own[i, 1, mine, :] = got1[u]

        @pl.when(core == 1)
        def _():
            for i, u in enumerate((u0, u1)):
                panels_own[i, :, mine, :] = got23[u]

    def col_of(yy, xx):
        return (yy * 4 + xx) * 2 + core

    def p1_copy(i, k, at):
        there = col_of(y, k) if i == 0 else col_of(k, x)
        source = pl.ds(pl.multiple_of(at * CHUNK, 8), CHUNK)
        return remote(
            panels_own.at[i, :, mine],
            panels_own.at[i, :, source],
            p1_send.at[i],
            p1_recv.at[i],
            row,
            there,
        )

    def p1_start():
        each(4, x, lambda k: p1_copy(0, k, chip).start())
        each(4, y, lambda k: p1_copy(1, k, chip).start())

    def p1_wait():
        for i in range(2):
            arrived(panels_own.at[i, :, pl.ds(0, 3 * CHUNK)], p1_recv.at[i])

    def p1_sent():
        for i in range(2):
            left(panels_own.at[i, :, pl.ds(0, 3 * CHUNK)], p1_send.at[i])

    def band(at):
        return panels_own.at[0, :, pl.ds(pl.multiple_of(at * 4 * CHUNK, 8), 4 * CHUNK)]

    def strip(yy, xx):
        return panels_own.at[
            1, :, pl.ds(pl.multiple_of((yy * 4 + xx) * CHUNK, 8), CHUNK)
        ]

    def p2_start():
        each(
            4,
            y,
            lambda k: remote(
                band(y), band(y), p2_send.at[0], p2_recv.at[0], row, col_of(k, x)
            ).start(),
        )

        def send(k):
            for yy in range(4):
                remote(
                    strip(yy, x),
                    strip(yy, x),
                    p2_send.at[1],
                    p2_recv.at[1],
                    row,
                    col_of(y, k),
                ).start()

        each(4, x, send)

    def p2_wait():
        for i in range(2):
            arrived(panels_own.at[i, :, pl.ds(0, 12 * CHUNK)], p2_recv.at[i])

    def p2_sent():
        for i in range(2):
            left(panels_own.at[i, :, pl.ds(0, 12 * CHUNK)], p2_send.at[i])

    def p3_copy():
        return remote(panels_own, panels_sib, p3_send, p3_recv, row, sibling)

    def share(ref, i, k):
        return ref.at[i, pl.ds(pl.multiple_of(k * SHARE, 8), SHARE)]

    def c1_copy(i, k):
        src = staged.at[0] if i == 0 else second
        return remote(
            src.at[pl.ds(pl.multiple_of(k * SHARE, 8), SHARE)],
            shares.at[i, row],
            c1_send.at[i],
            c1_recv.at[i],
            k,
            col,
        )

    here = pl.ds(pl.multiple_of(row * SHARE, 8), SHARE)

    def c1_start():
        for i in range(2):
            each(8, row, lambda k: c1_copy(i, k).start())
        shares[0, row] = staged[0, here, :]
        shares[1, row] = second[here, :]

    def c1_wait():
        for i in range(2):
            arrived(shares.at[i, pl.ds(0, 7)], c1_recv.at[i])

    def c1_sent():
        for i in range(2):
            left(shares.at[i, pl.ds(0, 7)], c1_send.at[i])

    def c2_start():
        turned[0, here, :] = shares[0, z0]
        turned[1, here, :] = shares[1, z1]
        each(
            8,
            row,
            lambda k: remote(
                turned.at[:, here],
                turned.at[:, here],
                c2_send,
                c2_recv,
                k,
                col,
            ).start(),
        )

    def c2_wait():
        arrived(turned.at[:, pl.ds(0, 7 * SHARE)], c2_recv)

    def c2_sent():
        left(turned.at[:, pl.ds(0, 7 * SHARE)], c2_send)

    a2a(0, got0, got0_sem, 0)
    stage(1)
    stage(2)
    stage(3)
    second[...] = staged[1 - same]
    c1_start()
    upper[...] = jnp.zeros_like(upper)
    inverse[...] = jnp.zeros_like(inverse)
    ework[...] = jnp.zeros_like(ework)

    @pl.when(core == 0)
    def _():
        a2a_wait(got0, got0_sem)
        zsend0[...] = got0[u0]
        z_start(zsend0, zgot0, z0_send, z0_recv)

    a2a(1, got1, got1_sem, 1)

    @pl.when(core == 0)
    def _():
        zsend1[...] = got0[u1]
        z_wait(zsend0, zgot0, z0_send, z0_recv)
        pivot[0, mine, :] = zgot0[z0]
        piv_start(0)
        z_start(zsend1, zgot1, z1_send, z1_recv)

    a2a23()

    @pl.when(core == 0)
    def _():
        piv_wait(0)
        sib_copy(0).start()

    @pl.when(core == 1)
    def _():
        sib_copy(0).wait_recv()

    work[0] = pivot[0]

    def comm(b):
        @pl.when(b == 1)
        def _():
            @pl.when(core == 0)
            def _():
                z_wait(zsend1, zgot1, z1_send, z1_recv)
                pivot[1, mine, :] = zgot1[z0]
                piv_start(1)
                a2a_wait(got1, got1_sem)
                weight = same.astype(F32)
                zsend2[...] = got0[u1] * weight + got1[u1] * (1.0 - weight)
                z_start(zsend2, zgot2, z2_send, z2_recv)

            @pl.when(core == 1)
            def _():
                a2a_wait(got23, got23_sem)

            panels_fill()
            p1_start()

        @pl.when(b == 2)
        def _():
            @pl.when(core == 0)
            def _():
                piv_wait(1)
                sib_copy(1).start()
                z_wait(zsend2, zgot2, z2_send, z2_recv)
                pivot[2, mine, :] = zgot2[z1]
                piv_start(2)

            p1_wait()
            p2_start()
            c1_wait()
            c2_start()

        @pl.when(b == 3)
        def _():
            @pl.when(core == 0)
            def _():
                piv_wait(2)
                sib_copy(2).start()

            @pl.when(core == 1)
            def _():
                sib_copy(1).wait_recv()
                sib_copy(2).wait_recv()

            cross[...] = product(inverse[0], pivot[1], ROWS_COLS)
            work[1] = pivot[2] - product(cross[...], cross[...], COLS_COLS)

        @pl.when(b == 5)
        def _():
            p2_wait()
            p3_copy().start()

    def block_step(b, carry):
        comm(b)
        s = b // 3
        part = b % 3
        r0 = pl.multiple_of(part * TILE, TILE)
        tile = pl.ds(r0, TILE)
        rows = [
            work[s, pl.ds(pl.multiple_of(r0 + 8 * q, 8), 8), tile] for q in range(16)
        ]
        up, inv = factor_tile(rows)
        for q in range(16):
            at = pl.ds(pl.multiple_of(r0 + 8 * q, 8), 8)
            upper[s, at, tile] = up[q]
            inverse[s, at, tile] = inv[q]
        small = inverse[s, tile, tile]
        lanes = lax.broadcasted_iota(jnp.int32, (TILE, BLOCK), 1)
        after = lanes >= r0 + TILE
        before = lanes < r0
        down = jnp.where(after, product(small, work[s, tile, :], ROWS_COLS), 0.0)
        behind = jnp.where(before, product(small, ework[s, tile, :], ROWS_COLS), 0.0)
        upper[s, tile, :] += down
        inverse[s, tile, :] += behind

        @pl.when(part < 2)
        def _():
            work[s] -= product(down, down, COLS_COLS)
            ework[s] -= product(down, inverse[s, tile, :], COLS_COLS)

        return carry

    lax.fori_loop(0, 6, block_step, 0)

    j = col_order[col]
    mask0 = flag((pattern[j, 0] == 1) & (j > 0))
    mask1 = flag((pattern[j, 1] == 1) & (j > 1))
    is0, is1 = flag(j == 0), flag(j == 1)
    rest_of = flag(j > 1)
    c2_wait()
    v0 = split(inverse[0])
    v1 = split(inverse[1])
    cr = split(cross[...])
    r0 = product3(v0, split(turned[0] * mask0), ROWS_COLS)
    r0s = split(r0)
    r1 = product3(
        v1, split((turned[1] - product3(cr, r0s, COLS_COLS)) * mask1), ROWS_COLS
    )
    r1s = split(r1)
    place = [jnp.int32(0)] * 4
    for slot in range(4):
        for b in range(4):
            place[b] = place[b] + (order[slot] == b).astype(jnp.int32) * slot

    def update(half, ref):
        for k in range(2):
            first = 1 - half
            i = row_order[row * 4 + first * order[k] + half * order[2 + k]]
            m0 = flag((pattern[i, 0] == 1) & (i > 0))
            m1 = flag((pattern[i, 1] == 1) & (i > 1))
            s0 = product3(split(ref[0, k] * m0), v0, ROWS_ROWS)
            s0s = split(s0)
            rest = (ref[1, k] - product3(s0s, cr, ROWS_COLS)) * m1
            s1 = product3(split(rest), v1, ROWS_ROWS)
            change = product3(s0s, r0s, ROWS_COLS) + product3(
                split(s1), r1s, ROWS_COLS
            )
            scaled[half * 2 + k] = is0 * s0 + is1 * s1 - rest_of * change

    update(core, panels_own)
    p3_copy().wait_recv()
    update(1 - core, panels_sib)

    factors = [upper[s].T * flag(j == s) for s in range(2)]
    for b in range(4):
        i = row_order[row * 4 + b]
        keep = flag((pattern[i, j] == 1) & (i >= j))
        center0, center1 = flag((i == 0) & (j == 0)), flag((i == 1) & (j == 1))
        value = matrix[b] * rest_of + scaled[place[b]]
        out[b] = value * keep + factors[0] * center0 + factors[1] * center1

    a2a_sent(0)
    a2a_sent(1)
    a2a23_sent()
    p1_sent()
    p2_sent()
    p3_copy().wait_send()
    c1_sent()
    c2_sent()

    @pl.when(core == 0)
    def _():
        z_sent(zsend0, zgot0, z0_send, z0_recv)
        z_sent(zsend1, zgot1, z1_send, z1_recv)
        z_sent(zsend2, zgot2, z2_send, z2_recv)
        for block in range(3):
            piv_sent(block)
            sib_copy(block).wait_send()


def body(matrix, pattern, row_order, col_order):
    block = (BLOCK, BLOCK)
    vmem = lambda *shape: pltpu.VMEM(shape, F32)
    dma = lambda *shape: pltpu.SemaphoreType.DMA(shape)
    return pl.pallas_call(
        kernel,
        out_shape=jax.ShapeDtypeStruct((4, *block), F32),
        in_specs=[pl.BlockSpec(memory_space=pltpu.SMEM)] * 3
        + [pl.BlockSpec(memory_space=pltpu.VMEM)],
        out_specs=pl.BlockSpec(memory_space=pltpu.VMEM),
        scratch_shapes=[
            vmem(4, *block),
            vmem(*block),
            vmem(32, CHUNK, BLOCK),
            vmem(32, CHUNK, BLOCK),
            vmem(32, 2, CHUNK, BLOCK),
            vmem(CHUNK, BLOCK),
            vmem(CHUNK, BLOCK),
            vmem(CHUNK, BLOCK),
            vmem(8, CHUNK, BLOCK),
            vmem(8, CHUNK, BLOCK),
            vmem(8, CHUNK, BLOCK),
            vmem(3, *block),
            vmem(2, *block),
            vmem(2, *block),
            vmem(2, *block),
            vmem(2, *block),
            vmem(*block),
            vmem(2, 2, *block),
            vmem(2, 2, *block),
            vmem(2, 8, SHARE, BLOCK),
            vmem(2, *block),
            vmem(4, *block),
            dma(3),
            pltpu.SemaphoreType.DMA,
            pltpu.SemaphoreType.DMA,
            pltpu.SemaphoreType.DMA,
            pltpu.SemaphoreType.DMA,
            pltpu.SemaphoreType.DMA,
            pltpu.SemaphoreType.DMA,
            pltpu.SemaphoreType.DMA,
            pltpu.SemaphoreType.DMA,
            pltpu.SemaphoreType.DMA,
            dma(3),
            dma(3),
            dma(3),
            dma(3),
            dma(2),
            dma(2),
            dma(2),
            dma(2),
            pltpu.SemaphoreType.DMA,
            pltpu.SemaphoreType.DMA,
            dma(2),
            dma(2),
            pltpu.SemaphoreType.DMA,
            pltpu.SemaphoreType.DMA,
        ],
        compiler_params=pltpu.CompilerParams(
            collective_id=0, has_side_effects=True, vmem_limit_bytes=60 * 2**20
        ),
    )(pattern, row_order, col_order, matrix.reshape(4, *block)).reshape(matrix.shape)


def solution(mesh):
    in_specs = (P("row", "col"), P(), P(), P())
    out_specs = P("row", "col")
    return jax.shard_map(body, mesh=mesh, in_specs=in_specs, out_specs=out_specs, check_vma=False)
```

```python
import jax
import jax.numpy as jnp
from jax import lax
from jax.experimental import pallas as pl
from jax.experimental.pallas import tpu as pltpu
from jax.sharding import PartitionSpec as P

BLOCK = 384
TILE = 128
CHUNK = BLOCK // 16
SHARE = BLOCK // 8
MESH = pl.DeviceIdType.MESH
EXACT = lax.Precision.HIGHEST
F32 = jnp.float32
BF16 = jnp.bfloat16
ROWS_COLS = ((1,), (0,))
COLS_COLS = ((0,), (0,))
ROWS_ROWS = ((1,), (1,))


def product(left, right, over):
    return lax.dot_general(
        left, right, (over, ((), ())), precision=EXACT, preferred_element_type=F32
    )


def split(value):
    high = value.astype(BF16)
    return high, (value - high.astype(F32)).astype(BF16)


def product3(pairs, over):
    left, right = [], []
    for a, b in pairs:
        left += [a[0], a[0], a[1]]
        right += [b[0], b[1], b[0]]
    return lax.dot_general(
        jnp.concatenate(left, axis=over[0][0]),
        jnp.concatenate(right, axis=over[1][0]),
        (over, ((), ())),
        preferred_element_type=F32,
    )


def lane(value, k):
    return jnp.broadcast_to(value[:, k : k + 1], (8, TILE))


def sublane(value, k):
    return jnp.broadcast_to(value[k : k + 1, :], (8, TILE))


def tree(terms):
    while len(terms) > 1:
        terms = [terms[i] + terms[i + 1] for i in range(0, len(terms), 2)]
    return terms[0]


def factor_tile(rows):
    lanes = lax.broadcasted_iota(jnp.int32, (8, TILE), 1)
    subs = lax.broadcasted_iota(jnp.int32, (8, TILE), 0)
    at = [subs == j for j in range(8)]
    a = list(rows)
    e = [jnp.where(lanes == subs + 8 * q, 1.0, 0.0).astype(F32) for q in range(16)]
    upper, inverse = [], []
    c = [lane(a[0], j) for j in range(8)]
    for p in range(16):
        ap, ep = a[p], e[p]
        ahead, beside, below = [], [], []
        if p < 15:
            ahead = [lane(ap, 8 * p + 8 + k) for k in range(8)]
            beside = [lane(a[p + 1], 8 * p + j) for j in range(8)]
            below = [lane(a[p + 1], 8 * p + 8 + k) for k in range(8)]
        fa, fe, pivots = ap, ep, c[0]
        for j in range(8):
            pivot = sublane(c[j], j)
            scale = 1.0 / pivot
            cj = jnp.where(at[j], -1.0, c[j])
            if j:
                fa = jnp.where(at[j], ap, fa)
                fe = jnp.where(at[j], ep, fe)
                pivots = jnp.where(at[j], pivot, pivots)

            def step(x):
                return jnp.where(at[j], 0.0, x) - cj * (sublane(x, j) * scale)

            for k in range(j + 1, 8):
                c[k] = step(c[k])
            ahead = [step(x) for x in ahead]
            ap, ep = step(ap), step(ep)
        c = [
            below[k] - tree([beside[j] * sublane(ahead[k], j) for j in range(8)])
            for k in range(len(ahead))
        ]
        root = lax.rsqrt(pivots)
        upper.append(jnp.where(lanes >= subs + 8 * p, fa * root, 0.0))
        inverse.append(fe * root)
        wa = [sublane(ap, j) for j in range(8)]
        we = [sublane(ep, j) for j in range(8)]
        for q in range(p + 1, 16):
            cq = beside if q == p + 1 else [lane(a[q], 8 * p + j) for j in range(8)]
            a[q] = a[q] - tree([cq[j] * wa[j] for j in range(8)])
            e[q] = e[q] - tree([cq[j] * we[j] for j in range(8)])
    return upper, inverse


def find(order_ref, wanted):
    place = jnp.int32(0)
    for t in range(32):
        place = place + (order_ref[t] == wanted).astype(jnp.int32) * t
    return jnp.minimum(place, 31)


def flag(condition):
    return condition.astype(jnp.int32).astype(F32)


def remote(src, dst, send, recv, row, col):
    return pltpu.make_async_remote_copy(
        src_ref=src,
        dst_ref=dst,
        send_sem=send,
        recv_sem=recv,
        device_id=(row, col),
        device_id_type=MESH,
    )


def each(count, me, do):
    for i in range(1, count):
        do((me + i) % count)


def kernel(
    pattern,
    row_order,
    col_order,
    matrix,
    out,
    staged,
    second,
    got0,
    got1,
    got23,
    zsend0,
    zsend1,
    zsend2,
    zgot0,
    zgot1,
    zgot2,
    pivot,
    work,
    ework,
    upper,
    inverse,
    cross,
    panels_own,
    panels_sib,
    shares,
    turned,
    scaled,
    a2a_send,
    got0_sem,
    got1_sem,
    got23_sem,
    z0_send,
    z0_recv,
    z1_send,
    z1_recv,
    z2_send,
    z2_recv,
    piv_send,
    piv_recv,
    sib_send,
    sib_recv,
    p1_send,
    p1_recv,
    p2_send,
    p2_recv,
    p3_send,
    p3_recv,
    c1_send,
    c1_recv,
    c2_send,
    c2_recv,
):
    row = lax.axis_index("row")
    col = lax.axis_index("col")
    chip, core = col // 2, col % 2
    y, x = chip // 4, chip % 4
    sibling = chip * 2 + (1 - core)

    barrier = pltpu.get_barrier_semaphore()

    def greet_col(k):
        pl.semaphore_signal(barrier, inc=1, device_id=(row, k), device_id_type=MESH)

    def greet_row(k):
        pl.semaphore_signal(barrier, inc=1, device_id=(k, col), device_id_type=MESH)

    each(32, col, greet_col)
    each(8, row, greet_row)

    place0, place1 = find(row_order, 0), find(row_order, 1)
    z0, z1 = place0 // 4, place1 // 4
    local0, local1 = place0 % 4, place1 % 4
    u0, u1 = find(col_order, 0), find(col_order, 1)
    same = (local0 == local1).astype(jnp.int32)
    step = (local1 - local0 + 4) % 4 + same
    order = [
        local0,
        (local0 + step) % 4,
        (local0 + 1 + (step == 1).astype(jnp.int32)) % 4,
        (local0 + 3 - (step == 3).astype(jnp.int32)) % 4,
    ]

    def stage(slot):
        staged[slot] = matrix[order[slot]]

    stage(0)
    pl.semaphore_wait(barrier, 31 + 7)

    def some(ref, count):
        return ref.at[pl.ds(0, count)]

    def arrived(ref, recv):
        remote(ref, ref, p3_send, recv, row, sibling).wait_recv()

    def left(ref, send):
        remote(ref, ref, send, p3_recv, row, sibling).wait_send()

    def a2a(slot, got, got_sem, sends):
        def piece(k):
            return staged.at[slot, pl.ds(pl.multiple_of(k * CHUNK, 8), CHUNK)]

        def send(k):
            remote(
                piece(k), got.at[col], a2a_send.at[sends], got_sem, row, 2 * k
            ).start()

        each(16, chip, send)

        @pl.when(core == 1)
        def _():
            send(chip)

        @pl.when(core == 0)
        def _():
            got[col] = staged[slot, pl.ds(pl.multiple_of(chip * CHUNK, 8), CHUNK), :]

    def a2a_wait(got, got_sem):
        arrived(some(got, 31), got_sem)

    def a2a_sent(sends):
        @pl.when(core == 0)
        def _():
            left(some(got0, 15), a2a_send.at[sends])

        @pl.when(core == 1)
        def _():
            left(some(got0, 16), a2a_send.at[sends])

    def piece23(k):
        return staged.at[pl.ds(2, 2), pl.ds(pl.multiple_of(k * CHUNK, 8), CHUNK)]

    def a2a23():
        def send(k):
            remote(
                piece23(k),
                got23.at[col],
                a2a_send.at[2],
                got23_sem,
                row,
                2 * k + 1,
            ).start()

        each(16, chip, send)

        @pl.when(core == 0)
        def _():
            send(chip)

        @pl.when(core == 1)
        def _():
            got23[col] = staged[
                pl.ds(2, 2), pl.ds(pl.multiple_of(chip * CHUNK, 8), CHUNK), :
            ]

    def a2a23_sent():
        @pl.when(core == 0)
        def _():
            left(some(got23, 16), a2a_send.at[2])

        @pl.when(core == 1)
        def _():
            left(some(got23, 15), a2a_send.at[2])

    def z_start(src, got, send_sem, recv_sem):
        each(
            8,
            row,
            lambda k: remote(src, got.at[row], send_sem, recv_sem, k, col).start(),
        )
        got[row] = src[...]

    def z_wait(src, got, send_sem, recv_sem):
        arrived(some(got, 7), recv_sem)

    def z_sent(src, got, send_sem, recv_sem):
        left(some(got, 7), send_sem)

    def chunk_of(block, k):
        return pivot.at[block, pl.ds(pl.multiple_of(k * CHUNK, 8), CHUNK)]

    def piv_start(block):
        def send(k):
            remote(
                chunk_of(block, chip),
                chunk_of(block, chip),
                piv_send.at[block],
                piv_recv.at[block],
                row,
                2 * k,
            ).start()

        each(16, chip, send)

    def piv_wait(block):
        arrived(pivot.at[block, pl.ds(0, 15 * CHUNK)], piv_recv.at[block])

    def piv_sent(block):
        left(pivot.at[block, pl.ds(0, 15 * CHUNK)], piv_send.at[block])

    def sib_copy(block):
        return remote(
            pivot.at[block],
            pivot.at[block],
            sib_send.at[block],
            sib_recv.at[block],
            row,
            sibling,
        )

    mine = pl.ds(pl.multiple_of(chip * CHUNK, 8), CHUNK)

    def panels_fill():
        @pl.when(core == 0)
        def _():
            for i, u in enumerate((u0, u1)):
                panels_own[i, 0, mine, :] = got0[u]
                panels_own[i, 1, mine, :] = got1[u]

        @pl.when(core == 1)
        def _():
            for i, u in enumerate((u0, u1)):
                panels_own[i, :, mine, :] = got23[u]

    def col_of(yy, xx):
        return (yy * 4 + xx) * 2 + core

    def p1_copy(i, k, at):
        there = col_of(y, k) if i == 0 else col_of(k, x)
        source = pl.ds(pl.multiple_of(at * CHUNK, 8), CHUNK)
        return remote(
            panels_own.at[i, :, mine],
            panels_own.at[i, :, source],
            p1_send.at[i],
            p1_recv.at[i],
            row,
            there,
        )

    def p1_start():
        each(4, x, lambda k: p1_copy(0, k, chip).start())
        each(4, y, lambda k: p1_copy(1, k, chip).start())

    def p1_wait():
        for i in range(2):
            arrived(panels_own.at[i, :, pl.ds(0, 3 * CHUNK)], p1_recv.at[i])

    def p1_sent():
        for i in range(2):
            left(panels_own.at[i, :, pl.ds(0, 3 * CHUNK)], p1_send.at[i])

    def band(at):
        return panels_own.at[0, :, pl.ds(pl.multiple_of(at * 4 * CHUNK, 8), 4 * CHUNK)]

    def strip(yy, xx):
        return panels_own.at[
            1, :, pl.ds(pl.multiple_of((yy * 4 + xx) * CHUNK, 8), CHUNK)
        ]

    def p2_start():
        each(
            4,
            y,
            lambda k: remote(
                band(y), band(y), p2_send.at[0], p2_recv.at[0], row, col_of(k, x)
            ).start(),
        )

        def send(k):
            for yy in range(4):
                remote(
                    strip(yy, x),
                    strip(yy, x),
                    p2_send.at[1],
                    p2_recv.at[1],
                    row,
                    col_of(y, k),
                ).start()

        each(4, x, send)

    def p2_wait():
        for i in range(2):
            arrived(panels_own.at[i, :, pl.ds(0, 12 * CHUNK)], p2_recv.at[i])

    def p2_sent():
        for i in range(2):
            left(panels_own.at[i, :, pl.ds(0, 12 * CHUNK)], p2_send.at[i])

    def p3_copy():
        return remote(panels_own, panels_sib, p3_send, p3_recv, row, sibling)

    def share(ref, i, k):
        return ref.at[i, pl.ds(pl.multiple_of(k * SHARE, 8), SHARE)]

    def c1_copy(i, k):
        src = staged.at[0] if i == 0 else second
        return remote(
            src.at[pl.ds(pl.multiple_of(k * SHARE, 8), SHARE)],
            shares.at[i, row],
            c1_send.at[i],
            c1_recv.at[i],
            k,
            col,
        )

    here = pl.ds(pl.multiple_of(row * SHARE, 8), SHARE)

    def c1_start(i):
        each(8, row, lambda k: c1_copy(i, k).start())
        shares[i, row] = staged[0, here, :] if i == 0 else second[here, :]

    def c1_wait():
        for i in range(2):
            arrived(shares.at[i, pl.ds(0, 7)], c1_recv.at[i])

    def c1_sent():
        for i in range(2):
            left(shares.at[i, pl.ds(0, 7)], c1_send.at[i])

    def c2_start():
        turned[0, here, :] = shares[0, z0]
        turned[1, here, :] = shares[1, z1]
        each(
            8,
            row,
            lambda k: remote(
                turned.at[:, here],
                turned.at[:, here],
                c2_send,
                c2_recv,
                k,
                col,
            ).start(),
        )

    def c2_wait():
        arrived(turned.at[:, pl.ds(0, 7 * SHARE)], c2_recv)

    def c2_sent():
        left(turned.at[:, pl.ds(0, 7 * SHARE)], c2_send)

    a2a(0, got0, got0_sem, 0)
    stage(1)
    stage(2)
    stage(3)
    second[...] = staged[1 - same]
    c1_start(0)

    @pl.when(core == 1)
    def _():
        c1_start(1)

    upper[...] = jnp.zeros_like(upper)
    inverse[...] = jnp.zeros_like(inverse)
    ework[...] = jnp.zeros_like(ework)

    @pl.when(core == 0)
    def _():
        a2a_wait(got0, got0_sem)
        zsend0[...] = got0[u0]
        z_start(zsend0, zgot0, z0_send, z0_recv)

    a2a(1, got1, got1_sem, 1)

    @pl.when(core == 0)
    def _():
        zsend1[...] = got0[u1]
        z_wait(zsend0, zgot0, z0_send, z0_recv)
        pivot[0, mine, :] = zgot0[z0]
        piv_start(0)
        z_start(zsend1, zgot1, z1_send, z1_recv)
        c1_start(1)

    a2a23()

    @pl.when(core == 0)
    def _():
        piv_wait(0)
        sib_copy(0).start()

    @pl.when(core == 1)
    def _():
        sib_copy(0).wait_recv()

    work[0] = pivot[0]

    def comm(b):
        @pl.when(b == 1)
        def _():
            @pl.when(core == 0)
            def _():
                z_wait(zsend1, zgot1, z1_send, z1_recv)
                pivot[1, mine, :] = zgot1[z0]
                piv_start(1)
                a2a_wait(got1, got1_sem)
                weight = same.astype(F32)
                zsend2[...] = got0[u1] * weight + got1[u1] * (1.0 - weight)
                z_start(zsend2, zgot2, z2_send, z2_recv)

        @pl.when(b == 2)
        def _():
            @pl.when(core == 0)
            def _():
                piv_wait(1)
                sib_copy(1).start()
                z_wait(zsend2, zgot2, z2_send, z2_recv)
                pivot[2, mine, :] = zgot2[z1]
                piv_start(2)

            @pl.when(core == 1)
            def _():
                a2a_wait(got23, got23_sem)

            panels_fill()
            p1_start()
            c1_wait()
            c2_start()

        @pl.when(b == 3)
        def _():
            @pl.when(core == 0)
            def _():
                piv_wait(2)
                sib_copy(2).start()

            @pl.when(core == 1)
            def _():
                sib_copy(1).wait_recv()
                sib_copy(2).wait_recv()

            p1_wait()
            p2_start()
            cross[...] = product(inverse[0], pivot[1], ROWS_COLS)
            work[1] = pivot[2] - product(cross[...], cross[...], COLS_COLS)

    def block_step(b, carry):
        comm(b)
        s = b // 3
        part = b % 3
        r0 = pl.multiple_of(part * TILE, TILE)
        tile = pl.ds(r0, TILE)
        rows = [
            work[s, pl.ds(pl.multiple_of(r0 + 8 * q, 8), 8), tile] for q in range(16)
        ]
        up, inv = factor_tile(rows)
        for q in range(16):
            at = pl.ds(pl.multiple_of(r0 + 8 * q, 8), 8)
            upper[s, at, tile] = up[q]
            inverse[s, at, tile] = inv[q]
        small = inverse[s, tile, tile]
        lanes = lax.broadcasted_iota(jnp.int32, (TILE, BLOCK), 1)
        after = lanes >= r0 + TILE
        before = lanes < r0
        down = jnp.where(after, product(small, work[s, tile, :], ROWS_COLS), 0.0)
        behind = jnp.where(before, product(small, ework[s, tile, :], ROWS_COLS), 0.0)
        upper[s, tile, :] += down
        inverse[s, tile, :] += behind

        @pl.when(part < 2)
        def _():
            work[s] -= product(down, down, COLS_COLS)
            ework[s] -= product(down, inverse[s, tile, :], COLS_COLS)

        return carry

    lax.fori_loop(0, 6, block_step, 0)

    j = col_order[col]
    mask0 = flag((pattern[j, 0] == 1) & (j > 0))
    mask1 = flag((pattern[j, 1] == 1) & (j > 1))
    is0, is1 = flag(j == 0), flag(j == 1)
    rest_of = flag(j > 1)
    v0 = split(inverse[0])
    v1 = split(inverse[1])
    cr = split(cross[...])

    place = [jnp.int32(0)] * 4
    for slot in range(4):
        for b in range(4):
            place[b] = place[b] + (order[slot] == b).astype(jnp.int32) * slot

    def scale(half, ref):
        for k in range(2):
            first = 1 - half
            i = row_order[row * 4 + first * order[k] + half * order[2 + k]]
            m0 = flag((pattern[i, 0] == 1) & (i > 0))
            m1 = flag((pattern[i, 1] == 1) & (i > 1))
            s0 = product3([(split(ref[0, k] * m0), v0)], ROWS_ROWS)
            rest = (ref[1, k] - product3([(split(s0), cr)], ROWS_COLS)) * m1
            scaled[half * 2 + k, 0] = s0
            scaled[half * 2 + k, 1] = product3([(split(rest), v1)], ROWS_ROWS)

    p2_wait()
    p3_copy().start()
    scale(core, panels_own)
    p3_copy().wait_recv()
    scale(1 - core, panels_sib)

    c2_wait()
    r0 = product3([(v0, split(turned[0] * mask0))], ROWS_COLS)
    r0s = split(r0)
    rest = (turned[1] - product3([(cr, r0s)], COLS_COLS)) * mask1
    r1s = split(product3([(v1, split(rest))], ROWS_COLS))

    factors = [upper[s].T * flag(j == s) for s in range(2)]
    for b in range(4):
        i = row_order[row * 4 + b]
        keep = flag((pattern[i, j] == 1) & (i >= j))
        center0, center1 = flag((i == 0) & (j == 0)), flag((i == 1) & (j == 1))
        s0, s1 = scaled[place[b], 0], scaled[place[b], 1]
        change = product3([(split(s0), r0s), (split(s1), r1s)], ROWS_COLS)
        value = (matrix[b] - change) * rest_of + s0 * is0 + s1 * is1
        out[b] = value * keep + factors[0] * center0 + factors[1] * center1

    a2a_sent(0)
    a2a_sent(1)
    a2a23_sent()
    p1_sent()
    p2_sent()
    p3_copy().wait_send()
    c1_sent()
    c2_sent()

    @pl.when(core == 0)
    def _():
        z_sent(zsend0, zgot0, z0_send, z0_recv)
        z_sent(zsend1, zgot1, z1_send, z1_recv)
        z_sent(zsend2, zgot2, z2_send, z2_recv)
        for block in range(3):
            piv_sent(block)
            sib_copy(block).wait_send()


def body(matrix, pattern, row_order, col_order):
    block = (BLOCK, BLOCK)
    vmem = lambda *shape: pltpu.VMEM(shape, F32)
    dma = lambda *shape: pltpu.SemaphoreType.DMA(shape)
    return pl.pallas_call(
        kernel,
        out_shape=jax.ShapeDtypeStruct((4, *block), F32),
        in_specs=[pl.BlockSpec(memory_space=pltpu.SMEM)] * 3
        + [pl.BlockSpec(memory_space=pltpu.VMEM)],
        out_specs=pl.BlockSpec(memory_space=pltpu.VMEM),
        scratch_shapes=[
            vmem(4, *block),
            vmem(*block),
            vmem(32, CHUNK, BLOCK),
            vmem(32, CHUNK, BLOCK),
            vmem(32, 2, CHUNK, BLOCK),
            vmem(CHUNK, BLOCK),
            vmem(CHUNK, BLOCK),
            vmem(CHUNK, BLOCK),
            vmem(8, CHUNK, BLOCK),
            vmem(8, CHUNK, BLOCK),
            vmem(8, CHUNK, BLOCK),
            vmem(3, *block),
            vmem(2, *block),
            vmem(2, *block),
            vmem(2, *block),
            vmem(2, *block),
            vmem(*block),
            vmem(2, 2, *block),
            vmem(2, 2, *block),
            vmem(2, 8, SHARE, BLOCK),
            vmem(2, *block),
            vmem(4, 2, *block),
            dma(3),
            pltpu.SemaphoreType.DMA,
            pltpu.SemaphoreType.DMA,
            pltpu.SemaphoreType.DMA,
            pltpu.SemaphoreType.DMA,
            pltpu.SemaphoreType.DMA,
            pltpu.SemaphoreType.DMA,
            pltpu.SemaphoreType.DMA,
            pltpu.SemaphoreType.DMA,
            pltpu.SemaphoreType.DMA,
            dma(3),
            dma(3),
            dma(3),
            dma(3),
            dma(2),
            dma(2),
            dma(2),
            dma(2),
            pltpu.SemaphoreType.DMA,
            pltpu.SemaphoreType.DMA,
            dma(2),
            dma(2),
            pltpu.SemaphoreType.DMA,
            pltpu.SemaphoreType.DMA,
        ],
        compiler_params=pltpu.CompilerParams(
            collective_id=0, has_side_effects=True, vmem_limit_bytes=60 * 2**20
        ),
    )(pattern, row_order, col_order, matrix.reshape(4, *block)).reshape(matrix.shape)


def solution(mesh):
    in_specs = (P("row", "col"), P(), P(), P())
    out_specs = P("row", "col")
    return jax.shard_map(body, mesh=mesh, in_specs=in_specs, out_specs=out_specs, check_vma=False)
```

```python
import jax
import jax.numpy as jnp
from jax import lax
from jax.experimental import pallas as pl
from jax.experimental.pallas import tpu as pltpu
from jax.sharding import PartitionSpec as P

BLOCK = 384
TILE = 128
CHUNK = BLOCK // 16
SHARE = BLOCK // 8
MESH = pl.DeviceIdType.MESH
EXACT = lax.Precision.HIGHEST
F32 = jnp.float32
BF16 = jnp.bfloat16
ROWS_COLS = ((1,), (0,))
COLS_COLS = ((0,), (0,))
ROWS_ROWS = ((1,), (1,))


def product(left, right, over):
    return lax.dot_general(
        left, right, (over, ((), ())), precision=EXACT, preferred_element_type=F32
    )


def split(value):
    high = value.astype(BF16)
    return high, (value - high.astype(F32)).astype(BF16)


def product3(pairs, over):
    left, right = [], []
    for a, b in pairs:
        left += [a[0], a[0], a[1]]
        right += [b[0], b[1], b[0]]
    return lax.dot_general(
        jnp.concatenate(left, axis=over[0][0]),
        jnp.concatenate(right, axis=over[1][0]),
        (over, ((), ())),
        preferred_element_type=F32,
    )


def lane(value, k):
    return jnp.broadcast_to(value[:, k : k + 1], (8, TILE))


def sublane(value, k):
    return jnp.broadcast_to(value[k : k + 1, :], (8, TILE))


def tree(terms):
    while len(terms) > 1:
        terms = [terms[i] + terms[i + 1] for i in range(0, len(terms), 2)]
    return terms[0]


def factor_tile(rows):
    lanes = lax.broadcasted_iota(jnp.int32, (8, TILE), 1)
    subs = lax.broadcasted_iota(jnp.int32, (8, TILE), 0)
    at = [subs == j for j in range(8)]
    a = list(rows)
    e = [jnp.where(lanes == subs + 8 * q, 1.0, 0.0).astype(F32) for q in range(16)]
    upper, inverse = [], []
    c = [lane(a[0], j) for j in range(8)]
    for p in range(16):
        ap, ep = a[p], e[p]
        ahead, beside, below = [], [], []
        if p < 15:
            ahead = [lane(ap, 8 * p + 8 + k) for k in range(8)]
            beside = [lane(a[p + 1], 8 * p + j) for j in range(8)]
            below = [lane(a[p + 1], 8 * p + 8 + k) for k in range(8)]
        fa, fe, pivots = ap, ep, c[0]
        for j in range(8):
            pivot = sublane(c[j], j)
            scale = 1.0 / pivot
            cj = jnp.where(at[j], -1.0, c[j])
            if j:
                fa = jnp.where(at[j], ap, fa)
                fe = jnp.where(at[j], ep, fe)
                pivots = jnp.where(at[j], pivot, pivots)

            def step(x):
                return jnp.where(at[j], 0.0, x) - cj * (sublane(x, j) * scale)

            for k in range(j + 1, 8):
                c[k] = step(c[k])
            ahead = [step(x) for x in ahead]
            ap, ep = step(ap), step(ep)
        c = [
            below[k] - tree([beside[j] * sublane(ahead[k], j) for j in range(8)])
            for k in range(len(ahead))
        ]
        root = lax.rsqrt(pivots)
        upper.append(jnp.where(lanes >= subs + 8 * p, fa * root, 0.0))
        inverse.append(fe * root)
        wa = [sublane(ap, j) for j in range(8)]
        we = [sublane(ep, j) for j in range(8)]
        for q in range(p + 1, 16):
            cq = beside if q == p + 1 else [lane(a[q], 8 * p + j) for j in range(8)]
            a[q] = a[q] - tree([cq[j] * wa[j] for j in range(8)])
            e[q] = e[q] - tree([cq[j] * we[j] for j in range(8)])
    return upper, inverse


def find(order_ref, wanted):
    place = jnp.int32(0)
    for t in range(32):
        place = place + (order_ref[t] == wanted).astype(jnp.int32) * t
    return jnp.minimum(place, 31)


def flag(condition):
    return condition.astype(jnp.int32).astype(F32)


def remote(src, dst, send, recv, row, col):
    return pltpu.make_async_remote_copy(
        src_ref=src,
        dst_ref=dst,
        send_sem=send,
        recv_sem=recv,
        device_id=(row, col),
        device_id_type=MESH,
    )


def each(count, me, do):
    for i in range(1, count):
        do((me + i) % count)


def kernel(
    pattern,
    row_order,
    col_order,
    matrix,
    out,
    staged,
    second,
    got0,
    got1,
    got23,
    zsend0,
    zsend1,
    zsend2,
    zgot0,
    zgot1,
    zgot2,
    pivot,
    work,
    ework,
    upper,
    inverse,
    cross,
    panels_own,
    panels_sib,
    shares,
    turned,
    scaled,
    a2a_send,
    got0_sem,
    got1_sem,
    got23_sem,
    z0_send,
    z0_recv,
    z1_send,
    z1_recv,
    z2_send,
    z2_recv,
    piv_send,
    piv_recv,
    sib_send,
    sib_recv,
    p1_send,
    p1_recv,
    p2_send,
    p2_recv,
    p3_send,
    p3_recv,
    c1_send,
    c1_recv,
    c2_send,
    c2_recv,
):
    row = lax.axis_index("row")
    col = lax.axis_index("col")
    chip, core = col // 2, col % 2
    y, x = chip // 4, chip % 4
    sibling = chip * 2 + (1 - core)

    barrier = pltpu.get_barrier_semaphore()

    def greet_col(k):
        pl.semaphore_signal(barrier, inc=1, device_id=(row, k), device_id_type=MESH)

    def greet_row(k):
        pl.semaphore_signal(barrier, inc=1, device_id=(k, col), device_id_type=MESH)

    each(32, col, greet_col)
    each(8, row, greet_row)

    place0, place1 = find(row_order, 0), find(row_order, 1)
    z0, z1 = place0 // 4, place1 // 4
    local0, local1 = place0 % 4, place1 % 4
    u0, u1 = find(col_order, 0), find(col_order, 1)
    same = (local0 == local1).astype(jnp.int32)
    step = (local1 - local0 + 4) % 4 + same
    order = [
        local0,
        (local0 + step) % 4,
        (local0 + 1 + (step == 1).astype(jnp.int32)) % 4,
        (local0 + 3 - (step == 3).astype(jnp.int32)) % 4,
    ]

    def stage(slot):
        staged[slot] = matrix[order[slot]]

    stage(0)
    pl.semaphore_wait(barrier, 31 + 7)

    def some(ref, count):
        return ref.at[pl.ds(0, count)]

    def arrived(ref, recv):
        remote(ref, ref, p3_send, recv, row, sibling).wait_recv()

    def left(ref, send):
        remote(ref, ref, send, p3_recv, row, sibling).wait_send()

    def a2a(slot, got, got_sem, sends):
        def piece(k):
            return staged.at[slot, pl.ds(pl.multiple_of(k * CHUNK, 8), CHUNK)]

        def send(k):
            remote(
                piece(k), got.at[col], a2a_send.at[sends], got_sem, row, 2 * k
            ).start()

        each(16, chip, send)

        @pl.when(core == 1)
        def _():
            send(chip)

        @pl.when(core == 0)
        def _():
            got[col] = staged[slot, pl.ds(pl.multiple_of(chip * CHUNK, 8), CHUNK), :]

    def a2a_wait(got, got_sem):
        arrived(some(got, 31), got_sem)

    def a2a_sent(sends):
        @pl.when(core == 0)
        def _():
            left(some(got0, 15), a2a_send.at[sends])

        @pl.when(core == 1)
        def _():
            left(some(got0, 16), a2a_send.at[sends])

    def piece23(k):
        return staged.at[pl.ds(2, 2), pl.ds(pl.multiple_of(k * CHUNK, 8), CHUNK)]

    def a2a23():
        def send(k):
            remote(
                piece23(k),
                got23.at[col],
                a2a_send.at[2],
                got23_sem,
                row,
                2 * k + 1,
            ).start()

        each(16, chip, send)

        @pl.when(core == 0)
        def _():
            send(chip)

        @pl.when(core == 1)
        def _():
            got23[col] = staged[
                pl.ds(2, 2), pl.ds(pl.multiple_of(chip * CHUNK, 8), CHUNK), :
            ]

    def a2a23_sent():
        @pl.when(core == 0)
        def _():
            left(some(got23, 16), a2a_send.at[2])

        @pl.when(core == 1)
        def _():
            left(some(got23, 15), a2a_send.at[2])

    def z_start(src, got, send_sem, recv_sem):
        each(
            8,
            row,
            lambda k: remote(src, got.at[row], send_sem, recv_sem, k, col).start(),
        )
        got[row] = src[...]

    def z_wait(src, got, send_sem, recv_sem):
        arrived(some(got, 7), recv_sem)

    def z_sent(src, got, send_sem, recv_sem):
        left(some(got, 7), send_sem)

    def chunk_of(block, k):
        return pivot.at[block, pl.ds(pl.multiple_of(k * CHUNK, 8), CHUNK)]

    def piv_start(block):
        def send(k):
            remote(
                chunk_of(block, chip),
                chunk_of(block, chip),
                piv_send.at[block],
                piv_recv.at[block],
                row,
                2 * k,
            ).start()

        each(16, chip, send)

    def piv_wait(block):
        arrived(pivot.at[block, pl.ds(0, 15 * CHUNK)], piv_recv.at[block])

    def piv_sent(block):
        left(pivot.at[block, pl.ds(0, 15 * CHUNK)], piv_send.at[block])

    def sib_copy(block):
        return remote(
            pivot.at[block],
            pivot.at[block],
            sib_send.at[block],
            sib_recv.at[block],
            row,
            sibling,
        )

    mine = pl.ds(pl.multiple_of(chip * CHUNK, 8), CHUNK)

    def panels_fill():
        @pl.when(core == 0)
        def _():
            for i, u in enumerate((u0, u1)):
                panels_own[i, 0, mine, :] = got0[u]
                panels_own[i, 1, mine, :] = got1[u]

        @pl.when(core == 1)
        def _():
            for i, u in enumerate((u0, u1)):
                panels_own[i, :, mine, :] = got23[u]

    def col_of(yy, xx):
        return (yy * 4 + xx) * 2 + core

    def p1_copy(i, k, at):
        there = col_of(y, k) if i == 0 else col_of(k, x)
        source = pl.ds(pl.multiple_of(at * CHUNK, 8), CHUNK)
        return remote(
            panels_own.at[i, :, mine],
            panels_own.at[i, :, source],
            p1_send.at[i],
            p1_recv.at[i],
            row,
            there,
        )

    def p1_start():
        each(4, x, lambda k: p1_copy(0, k, chip).start())
        each(4, y, lambda k: p1_copy(1, k, chip).start())

    def p1_wait():
        for i in range(2):
            arrived(panels_own.at[i, :, pl.ds(0, 3 * CHUNK)], p1_recv.at[i])

    def p1_sent():
        for i in range(2):
            left(panels_own.at[i, :, pl.ds(0, 3 * CHUNK)], p1_send.at[i])

    def band(at):
        return panels_own.at[0, :, pl.ds(pl.multiple_of(at * 4 * CHUNK, 8), 4 * CHUNK)]

    def strip(yy, xx):
        return panels_own.at[
            1, :, pl.ds(pl.multiple_of((yy * 4 + xx) * CHUNK, 8), CHUNK)
        ]

    def p2_start():
        each(
            4,
            y,
            lambda k: remote(
                band(y), band(y), p2_send.at[0], p2_recv.at[0], row, col_of(k, x)
            ).start(),
        )

        def send(k):
            for yy in range(4):
                remote(
                    strip(yy, x),
                    strip(yy, x),
                    p2_send.at[1],
                    p2_recv.at[1],
                    row,
                    col_of(y, k),
                ).start()

        each(4, x, send)

    def p2_wait():
        for i in range(2):
            arrived(panels_own.at[i, :, pl.ds(0, 12 * CHUNK)], p2_recv.at[i])

    def p2_sent():
        for i in range(2):
            left(panels_own.at[i, :, pl.ds(0, 12 * CHUNK)], p2_send.at[i])

    def p3_copy():
        return remote(panels_own, panels_sib, p3_send, p3_recv, row, sibling)

    def share(ref, i, k):
        return ref.at[i, pl.ds(pl.multiple_of(k * SHARE, 8), SHARE)]

    def c1_copy(i, k):
        src = staged.at[0] if i == 0 else second
        return remote(
            src.at[pl.ds(pl.multiple_of(k * SHARE, 8), SHARE)],
            shares.at[i, row],
            c1_send.at[i],
            c1_recv.at[i],
            k,
            col,
        )

    here = pl.ds(pl.multiple_of(row * SHARE, 8), SHARE)

    def c1_start(i):
        each(8, row, lambda k: c1_copy(i, k).start())
        shares[i, row] = staged[0, here, :] if i == 0 else second[here, :]

    def c1_wait():
        for i in range(2):
            arrived(shares.at[i, pl.ds(0, 7)], c1_recv.at[i])

    def c1_sent():
        for i in range(2):
            left(shares.at[i, pl.ds(0, 7)], c1_send.at[i])

    def c2_start():
        turned[0, here, :] = shares[0, z0]
        turned[1, here, :] = shares[1, z1]
        each(
            8,
            row,
            lambda k: remote(
                turned.at[:, here],
                turned.at[:, here],
                c2_send,
                c2_recv,
                k,
                col,
            ).start(),
        )

    def c2_wait():
        arrived(turned.at[:, pl.ds(0, 7 * SHARE)], c2_recv)

    def c2_sent():
        left(turned.at[:, pl.ds(0, 7 * SHARE)], c2_send)

    a2a(0, got0, got0_sem, 0)
    stage(1)
    stage(2)
    stage(3)
    second[...] = staged[1 - same]
    c1_start(0)
    upper[...] = jnp.zeros_like(upper)
    inverse[...] = jnp.zeros_like(inverse)
    ework[...] = jnp.zeros_like(ework)

    @pl.when(core == 0)
    def _():
        a2a_wait(got0, got0_sem)
        zsend0[...] = got0[u0]
        z_start(zsend0, zgot0, z0_send, z0_recv)

    a2a(1, got1, got1_sem, 1)

    @pl.when(core == 0)
    def _():
        zsend1[...] = got0[u1]
        z_wait(zsend0, zgot0, z0_send, z0_recv)
        pivot[0, mine, :] = zgot0[z0]
        piv_start(0)
        z_start(zsend1, zgot1, z1_send, z1_recv)
        c1_start(1)

    a2a23()

    @pl.when(core == 0)
    def _():
        piv_wait(0)
        sib_copy(0).start()

    @pl.when(core == 1)
    def _():
        sib_copy(0).wait_recv()
        c1_start(1)

    work[0] = pivot[0]

    def comm(b):
        @pl.when(b == 1)
        def _():
            @pl.when(core == 0)
            def _():
                z_wait(zsend1, zgot1, z1_send, z1_recv)
                pivot[1, mine, :] = zgot1[z0]
                piv_start(1)
                a2a_wait(got1, got1_sem)
                weight = same.astype(F32)
                zsend2[...] = got0[u1] * weight + got1[u1] * (1.0 - weight)
                z_start(zsend2, zgot2, z2_send, z2_recv)

        @pl.when(b == 2)
        def _():
            @pl.when(core == 0)
            def _():
                piv_wait(1)
                sib_copy(1).start()
                z_wait(zsend2, zgot2, z2_send, z2_recv)
                pivot[2, mine, :] = zgot2[z1]
                piv_start(2)

            @pl.when(core == 1)
            def _():
                a2a_wait(got23, got23_sem)

            panels_fill()
            p1_start()
            c1_wait()
            c2_start()

        @pl.when(b == 3)
        def _():
            @pl.when(core == 0)
            def _():
                piv_wait(2)
                sib_copy(2).start()

            @pl.when(core == 1)
            def _():
                sib_copy(1).wait_recv()
                sib_copy(2).wait_recv()

            p1_wait()
            p2_start()
            cross[...] = product(inverse[0], pivot[1], ROWS_COLS)
            work[1] = pivot[2] - product(cross[...], cross[...], COLS_COLS)

    def block_step(b, carry):
        comm(b)
        s = b // 3
        part = b % 3
        r0 = pl.multiple_of(part * TILE, TILE)
        tile = pl.ds(r0, TILE)
        rows = [
            work[s, pl.ds(pl.multiple_of(r0 + 8 * q, 8), 8), tile] for q in range(16)
        ]
        up, inv = factor_tile(rows)
        for q in range(16):
            at = pl.ds(pl.multiple_of(r0 + 8 * q, 8), 8)
            upper[s, at, tile] = up[q]
            inverse[s, at, tile] = inv[q]
        small = inverse[s, tile, tile]
        lanes = lax.broadcasted_iota(jnp.int32, (TILE, BLOCK), 1)
        after = lanes >= r0 + TILE
        before = lanes < r0
        down = jnp.where(after, product(small, work[s, tile, :], ROWS_COLS), 0.0)
        behind = jnp.where(before, product(small, ework[s, tile, :], ROWS_COLS), 0.0)
        upper[s, tile, :] += down
        inverse[s, tile, :] += behind

        @pl.when(part < 2)
        def _():
            work[s] -= product(down, down, COLS_COLS)
            ework[s] -= product(down, inverse[s, tile, :], COLS_COLS)

        return carry

    lax.fori_loop(0, 6, block_step, 0)

    j = col_order[col]
    mask0 = flag((pattern[j, 0] == 1) & (j > 0))
    mask1 = flag((pattern[j, 1] == 1) & (j > 1))
    is0, is1 = flag(j == 0), flag(j == 1)
    rest_of = flag(j > 1)
    v0 = split(inverse[0])
    v1 = split(inverse[1])
    cr = split(cross[...])

    place = [jnp.int32(0)] * 4
    for slot in range(4):
        for b in range(4):
            place[b] = place[b] + (order[slot] == b).astype(jnp.int32) * slot

    def scale(half, ref):
        for k in range(2):
            first = 1 - half
            i = row_order[row * 4 + first * order[k] + half * order[2 + k]]
            m0 = flag((pattern[i, 0] == 1) & (i > 0))
            m1 = flag((pattern[i, 1] == 1) & (i > 1))
            s0 = product3([(split(ref[0, k] * m0), v0)], ROWS_ROWS)
            rest = (ref[1, k] - product3([(split(s0), cr)], ROWS_COLS)) * m1
            scaled[half * 2 + k, 0] = s0
            scaled[half * 2 + k, 1] = product3([(split(rest), v1)], ROWS_ROWS)

    p2_wait()
    p3_copy().start()
    scale(core, panels_own)
    p3_copy().wait_recv()
    scale(1 - core, panels_sib)

    c2_wait()
    r0 = product3([(v0, split(turned[0] * mask0))], ROWS_COLS)
    r0s = split(r0)
    rest = (turned[1] - product3([(cr, r0s)], COLS_COLS)) * mask1
    r1s = split(product3([(v1, split(rest))], ROWS_COLS))

    factors = [upper[s].T * flag(j == s) for s in range(2)]
    for b in range(4):
        i = row_order[row * 4 + b]
        keep = flag((pattern[i, j] == 1) & (i >= j))
        center0, center1 = flag((i == 0) & (j == 0)), flag((i == 1) & (j == 1))
        s0, s1 = scaled[place[b], 0], scaled[place[b], 1]
        change = product3([(split(s0), r0s), (split(s1), r1s)], ROWS_COLS)
        value = (matrix[b] - change) * rest_of + s0 * is0 + s1 * is1
        out[b] = value * keep + factors[0] * center0 + factors[1] * center1

    a2a_sent(0)
    a2a_sent(1)
    a2a23_sent()
    p1_sent()
    p2_sent()
    p3_copy().wait_send()
    c1_sent()
    c2_sent()

    @pl.when(core == 0)
    def _():
        z_sent(zsend0, zgot0, z0_send, z0_recv)
        z_sent(zsend1, zgot1, z1_send, z1_recv)
        z_sent(zsend2, zgot2, z2_send, z2_recv)
        for block in range(3):
            piv_sent(block)
            sib_copy(block).wait_send()


def body(matrix, pattern, row_order, col_order):
    block = (BLOCK, BLOCK)
    vmem = lambda *shape: pltpu.VMEM(shape, F32)
    dma = lambda *shape: pltpu.SemaphoreType.DMA(shape)
    return pl.pallas_call(
        kernel,
        out_shape=jax.ShapeDtypeStruct((4, *block), F32),
        in_specs=[pl.BlockSpec(memory_space=pltpu.SMEM)] * 3
        + [pl.BlockSpec(memory_space=pltpu.VMEM)],
        out_specs=pl.BlockSpec(memory_space=pltpu.VMEM),
        scratch_shapes=[
            vmem(4, *block),
            vmem(*block),
            vmem(32, CHUNK, BLOCK),
            vmem(32, CHUNK, BLOCK),
            vmem(32, 2, CHUNK, BLOCK),
            vmem(CHUNK, BLOCK),
            vmem(CHUNK, BLOCK),
            vmem(CHUNK, BLOCK),
            vmem(8, CHUNK, BLOCK),
            vmem(8, CHUNK, BLOCK),
            vmem(8, CHUNK, BLOCK),
            vmem(3, *block),
            vmem(2, *block),
            vmem(2, *block),
            vmem(2, *block),
            vmem(2, *block),
            vmem(*block),
            vmem(2, 2, *block),
            vmem(2, 2, *block),
            vmem(2, 8, SHARE, BLOCK),
            vmem(2, *block),
            vmem(4, 2, *block),
            dma(3),
            pltpu.SemaphoreType.DMA,
            pltpu.SemaphoreType.DMA,
            pltpu.SemaphoreType.DMA,
            pltpu.SemaphoreType.DMA,
            pltpu.SemaphoreType.DMA,
            pltpu.SemaphoreType.DMA,
            pltpu.SemaphoreType.DMA,
            pltpu.SemaphoreType.DMA,
            pltpu.SemaphoreType.DMA,
            dma(3),
            dma(3),
            dma(3),
            dma(3),
            dma(2),
            dma(2),
            dma(2),
            dma(2),
            pltpu.SemaphoreType.DMA,
            pltpu.SemaphoreType.DMA,
            dma(2),
            dma(2),
            pltpu.SemaphoreType.DMA,
            pltpu.SemaphoreType.DMA,
        ],
        compiler_params=pltpu.CompilerParams(
            collective_id=0, has_side_effects=True, vmem_limit_bytes=60 * 2**20
        ),
    )(pattern, row_order, col_order, matrix.reshape(4, *block)).reshape(matrix.shape)


def solution(mesh):
    in_specs = (P("row", "col"), P(), P(), P())
    out_specs = P("row", "col")
    return jax.shard_map(body, mesh=mesh, in_specs=in_specs, out_specs=out_specs, check_vma=False)
```

```python
import jax
import jax.numpy as jnp
from jax import lax
from jax.experimental import pallas as pl
from jax.experimental.pallas import tpu as pltpu
from jax.sharding import PartitionSpec as P

BLOCK = 384
TILE = 128
CHUNK = BLOCK // 16
SHARE = BLOCK // 8
MESH = pl.DeviceIdType.MESH
EXACT = lax.Precision.HIGHEST
F32 = jnp.float32
BF16 = jnp.bfloat16
ROWS_COLS = ((1,), (0,))
COLS_COLS = ((0,), (0,))
ROWS_ROWS = ((1,), (1,))


def product(left, right, over):
    return lax.dot_general(
        left, right, (over, ((), ())), precision=EXACT, preferred_element_type=F32
    )


def split(value):
    high = value.astype(BF16)
    return high, (value - high.astype(F32)).astype(BF16)


def product3(pairs, over):
    left, right = [], []
    for a, b in pairs:
        left += [a[0], a[0], a[1]]
        right += [b[0], b[1], b[0]]
    return lax.dot_general(
        jnp.concatenate(left, axis=over[0][0]),
        jnp.concatenate(right, axis=over[1][0]),
        (over, ((), ())),
        preferred_element_type=F32,
    )


def lane(value, k):
    return jnp.broadcast_to(value[:, k : k + 1], (8, TILE))


def sublane(value, k):
    return jnp.broadcast_to(value[k : k + 1, :], (8, TILE))


def tree(terms):
    while len(terms) > 1:
        terms = [terms[i] + terms[i + 1] for i in range(0, len(terms), 2)]
    return terms[0]


def factor_tile(rows):
    lanes = lax.broadcasted_iota(jnp.int32, (8, TILE), 1)
    subs = lax.broadcasted_iota(jnp.int32, (8, TILE), 0)
    at = [subs == j for j in range(8)]
    a = list(rows)
    e = [jnp.where(lanes == subs + 8 * q, 1.0, 0.0).astype(F32) for q in range(16)]
    upper, inverse = [], []
    c = [lane(a[0], j) for j in range(8)]
    for p in range(16):
        ap, ep = a[p], e[p]
        ahead, beside, below = [], [], []
        if p < 15:
            ahead = [lane(ap, 8 * p + 8 + k) for k in range(8)]
            beside = [lane(a[p + 1], 8 * p + j) for j in range(8)]
            below = [lane(a[p + 1], 8 * p + 8 + k) for k in range(8)]
        fa, fe, pivots = ap, ep, c[0]
        for j in range(8):
            pivot = sublane(c[j], j)
            scale = 1.0 / pivot
            cj = jnp.where(at[j], -1.0, c[j])
            if j:
                fa = jnp.where(at[j], ap, fa)
                fe = jnp.where(at[j], ep, fe)
                pivots = jnp.where(at[j], pivot, pivots)

            def step(x):
                return jnp.where(at[j], 0.0, x) - cj * (sublane(x, j) * scale)

            for k in range(j + 1, 8):
                c[k] = step(c[k])
            ahead = [step(x) for x in ahead]
            ap, ep = step(ap), step(ep)
        c = [
            below[k] - tree([beside[j] * sublane(ahead[k], j) for j in range(8)])
            for k in range(len(ahead))
        ]
        root = lax.rsqrt(pivots)
        upper.append(jnp.where(lanes >= subs + 8 * p, fa * root, 0.0))
        inverse.append(fe * root)
        wa = [sublane(ap, j) for j in range(8)]
        we = [sublane(ep, j) for j in range(8)]
        for q in range(p + 1, 16):
            cq = beside if q == p + 1 else [lane(a[q], 8 * p + j) for j in range(8)]
            a[q] = a[q] - tree([cq[j] * wa[j] for j in range(8)])
            e[q] = e[q] - tree([cq[j] * we[j] for j in range(8)])
    return upper, inverse


def find(order_ref, wanted):
    place = jnp.int32(0)
    for t in range(32):
        place = place + (order_ref[t] == wanted).astype(jnp.int32) * t
    return jnp.minimum(place, 31)


def flag(condition):
    return condition.astype(jnp.int32).astype(F32)


def remote(src, dst, send, recv, row, col):
    return pltpu.make_async_remote_copy(
        src_ref=src,
        dst_ref=dst,
        send_sem=send,
        recv_sem=recv,
        device_id=(row, col),
        device_id_type=MESH,
    )


def each(count, me, do):
    for i in range(1, count):
        do((me + i) % count)


def kernel(
    pattern,
    row_order,
    col_order,
    matrix_hbm,
    out_hbm,
    matrix,
    out,
    load_sem,
    store_sem,
    staged,
    second,
    got0,
    got1,
    got23,
    zsend0,
    zsend1,
    zsend2,
    zgot0,
    zgot1,
    zgot2,
    pivot,
    work,
    ework,
    upper,
    inverse,
    cross,
    panels_own,
    panels_sib,
    shares,
    turned,
    scaled,
    a2a_send,
    got0_sem,
    got1_sem,
    got23_sem,
    z0_send,
    z0_recv,
    z1_send,
    z1_recv,
    z2_send,
    z2_recv,
    piv_send,
    piv_recv,
    sib_send,
    sib_recv,
    p1_send,
    p1_recv,
    p2_send,
    p2_recv,
    p3_send,
    p3_recv,
    c1_send,
    c1_recv,
    c2_send,
    c2_recv,
):
    row = lax.axis_index("row")
    col = lax.axis_index("col")
    chip, core = col // 2, col % 2
    y, x = chip // 4, chip % 4
    sibling = chip * 2 + (1 - core)

    barrier = pltpu.get_barrier_semaphore()

    def greet_col(k):
        pl.semaphore_signal(barrier, inc=1, device_id=(row, k), device_id_type=MESH)

    def greet_row(k):
        pl.semaphore_signal(barrier, inc=1, device_id=(k, col), device_id_type=MESH)

    each(32, col, greet_col)
    each(8, row, greet_row)
    load = pltpu.make_async_copy(matrix_hbm, matrix, load_sem)
    load.start()

    place0, place1 = find(row_order, 0), find(row_order, 1)
    z0, z1 = place0 // 4, place1 // 4
    local0, local1 = place0 % 4, place1 % 4
    u0, u1 = find(col_order, 0), find(col_order, 1)
    same = (local0 == local1).astype(jnp.int32)
    step = (local1 - local0 + 4) % 4 + same
    order = [
        local0,
        (local0 + step) % 4,
        (local0 + 1 + (step == 1).astype(jnp.int32)) % 4,
        (local0 + 3 - (step == 3).astype(jnp.int32)) % 4,
    ]

    def stage(slot):
        staged[slot] = matrix[order[slot]]

    load.wait()
    stage(0)
    pl.semaphore_wait(barrier, 31 + 7)

    def some(ref, count):
        return ref.at[pl.ds(0, count)]

    def arrived(ref, recv):
        remote(ref, ref, p3_send, recv, row, sibling).wait_recv()

    def left(ref, send):
        remote(ref, ref, send, p3_recv, row, sibling).wait_send()

    def a2a(slot, got, got_sem, sends):
        def piece(k):
            return staged.at[slot, pl.ds(pl.multiple_of(k * CHUNK, 8), CHUNK)]

        def send(k):
            remote(
                piece(k), got.at[col], a2a_send.at[sends], got_sem, row, 2 * k
            ).start()

        each(16, chip, send)

        @pl.when(core == 1)
        def _():
            send(chip)

        @pl.when(core == 0)
        def _():
            got[col] = staged[slot, pl.ds(pl.multiple_of(chip * CHUNK, 8), CHUNK), :]

    def a2a_wait(got, got_sem):
        arrived(some(got, 31), got_sem)

    def a2a_sent(sends):
        @pl.when(core == 0)
        def _():
            left(some(got0, 15), a2a_send.at[sends])

        @pl.when(core == 1)
        def _():
            left(some(got0, 16), a2a_send.at[sends])

    def piece23(k):
        return staged.at[pl.ds(2, 2), pl.ds(pl.multiple_of(k * CHUNK, 8), CHUNK)]

    def a2a23():
        def send(k):
            remote(
                piece23(k),
                got23.at[col],
                a2a_send.at[2],
                got23_sem,
                row,
                2 * k + 1,
            ).start()

        each(16, chip, send)

        @pl.when(core == 0)
        def _():
            send(chip)

        @pl.when(core == 1)
        def _():
            got23[col] = staged[
                pl.ds(2, 2), pl.ds(pl.multiple_of(chip * CHUNK, 8), CHUNK), :
            ]

    def a2a23_sent():
        @pl.when(core == 0)
        def _():
            left(some(got23, 16), a2a_send.at[2])

        @pl.when(core == 1)
        def _():
            left(some(got23, 15), a2a_send.at[2])

    def z_start(src, got, send_sem, recv_sem):
        each(
            8,
            row,
            lambda k: remote(src, got.at[row], send_sem, recv_sem, k, col).start(),
        )
        got[row] = src[...]

    def z_wait(src, got, send_sem, recv_sem):
        arrived(some(got, 7), recv_sem)

    def z_sent(src, got, send_sem, recv_sem):
        left(some(got, 7), send_sem)

    def chunk_of(block, k):
        return pivot.at[block, pl.ds(pl.multiple_of(k * CHUNK, 8), CHUNK)]

    def piv_start(block):
        def send(k):
            remote(
                chunk_of(block, chip),
                chunk_of(block, chip),
                piv_send.at[block],
                piv_recv.at[block],
                row,
                2 * k,
            ).start()

        each(16, chip, send)

    def piv_wait(block):
        arrived(pivot.at[block, pl.ds(0, 15 * CHUNK)], piv_recv.at[block])

    def piv_sent(block):
        left(pivot.at[block, pl.ds(0, 15 * CHUNK)], piv_send.at[block])

    def sib_copy(block):
        return remote(
            pivot.at[block],
            pivot.at[block],
            sib_send.at[block],
            sib_recv.at[block],
            row,
            sibling,
        )

    mine = pl.ds(pl.multiple_of(chip * CHUNK, 8), CHUNK)

    def panels_fill():
        @pl.when(core == 0)
        def _():
            for i, u in enumerate((u0, u1)):
                panels_own[i, 0, mine, :] = got0[u]
                panels_own[i, 1, mine, :] = got1[u]

        @pl.when(core == 1)
        def _():
            for i, u in enumerate((u0, u1)):
                panels_own[i, :, mine, :] = got23[u]

    def col_of(yy, xx):
        return (yy * 4 + xx) * 2 + core

    def p1_copy(i, k, at):
        there = col_of(y, k) if i == 0 else col_of(k, x)
        source = pl.ds(pl.multiple_of(at * CHUNK, 8), CHUNK)
        return remote(
            panels_own.at[i, :, mine],
            panels_own.at[i, :, source],
            p1_send.at[i],
            p1_recv.at[i],
            row,
            there,
        )

    def p1_start():
        each(4, x, lambda k: p1_copy(0, k, chip).start())
        each(4, y, lambda k: p1_copy(1, k, chip).start())

    def p1_wait():
        for i in range(2):
            arrived(panels_own.at[i, :, pl.ds(0, 3 * CHUNK)], p1_recv.at[i])

    def p1_sent():
        for i in range(2):
            left(panels_own.at[i, :, pl.ds(0, 3 * CHUNK)], p1_send.at[i])

    def band(at):
        return panels_own.at[0, :, pl.ds(pl.multiple_of(at * 4 * CHUNK, 8), 4 * CHUNK)]

    def strip(yy, xx):
        return panels_own.at[
            1, :, pl.ds(pl.multiple_of((yy * 4 + xx) * CHUNK, 8), CHUNK)
        ]

    def p2_start():
        each(
            4,
            y,
            lambda k: remote(
                band(y), band(y), p2_send.at[0], p2_recv.at[0], row, col_of(k, x)
            ).start(),
        )

        def send(k):
            for yy in range(4):
                remote(
                    strip(yy, x),
                    strip(yy, x),
                    p2_send.at[1],
                    p2_recv.at[1],
                    row,
                    col_of(y, k),
                ).start()

        each(4, x, send)

    def p2_wait():
        for i in range(2):
            arrived(panels_own.at[i, :, pl.ds(0, 12 * CHUNK)], p2_recv.at[i])

    def p2_sent():
        for i in range(2):
            left(panels_own.at[i, :, pl.ds(0, 12 * CHUNK)], p2_send.at[i])

    def p3_copy():
        return remote(panels_own, panels_sib, p3_send, p3_recv, row, sibling)

    def share(ref, i, k):
        return ref.at[i, pl.ds(pl.multiple_of(k * SHARE, 8), SHARE)]

    def c1_copy(i, k):
        src = staged.at[0] if i == 0 else second
        return remote(
            src.at[pl.ds(pl.multiple_of(k * SHARE, 8), SHARE)],
            shares.at[i, row],
            c1_send.at[i],
            c1_recv.at[i],
            k,
            col,
        )

    here = pl.ds(pl.multiple_of(row * SHARE, 8), SHARE)

    def c1_start(i):
        each(8, row, lambda k: c1_copy(i, k).start())
        shares[i, row] = staged[0, here, :] if i == 0 else second[here, :]

    def c1_wait():
        for i in range(2):
            arrived(shares.at[i, pl.ds(0, 7)], c1_recv.at[i])

    def c1_sent():
        for i in range(2):
            left(shares.at[i, pl.ds(0, 7)], c1_send.at[i])

    def c2_start():
        turned[0, here, :] = shares[0, z0]
        turned[1, here, :] = shares[1, z1]
        each(
            8,
            row,
            lambda k: remote(
                turned.at[:, here],
                turned.at[:, here],
                c2_send,
                c2_recv,
                k,
                col,
            ).start(),
        )

    def c2_wait():
        arrived(turned.at[:, pl.ds(0, 7 * SHARE)], c2_recv)

    def c2_sent():
        left(turned.at[:, pl.ds(0, 7 * SHARE)], c2_send)

    a2a(0, got0, got0_sem, 0)
    stage(1)
    stage(2)
    stage(3)
    second[...] = staged[1 - same]
    c1_start(0)
    upper[...] = jnp.zeros_like(upper)
    inverse[...] = jnp.zeros_like(inverse)
    ework[...] = jnp.zeros_like(ework)

    @pl.when(core == 0)
    def _():
        a2a_wait(got0, got0_sem)
        zsend0[...] = got0[u0]
        z_start(zsend0, zgot0, z0_send, z0_recv)

    a2a(1, got1, got1_sem, 1)

    @pl.when(core == 0)
    def _():
        zsend1[...] = got0[u1]
        z_wait(zsend0, zgot0, z0_send, z0_recv)
        pivot[0, mine, :] = zgot0[z0]
        piv_start(0)
        z_start(zsend1, zgot1, z1_send, z1_recv)
        c1_start(1)

    a2a23()

    @pl.when(core == 0)
    def _():
        piv_wait(0)
        sib_copy(0).start()

    @pl.when(core == 1)
    def _():
        sib_copy(0).wait_recv()
        c1_start(1)

    work[0] = pivot[0]

    def comm(b):
        @pl.when(b == 1)
        def _():
            @pl.when(core == 0)
            def _():
                z_wait(zsend1, zgot1, z1_send, z1_recv)
                pivot[1, mine, :] = zgot1[z0]
                piv_start(1)
                a2a_wait(got1, got1_sem)
                weight = same.astype(F32)
                zsend2[...] = got0[u1] * weight + got1[u1] * (1.0 - weight)
                z_start(zsend2, zgot2, z2_send, z2_recv)

        @pl.when(b == 2)
        def _():
            @pl.when(core == 0)
            def _():
                piv_wait(1)
                sib_copy(1).start()
                z_wait(zsend2, zgot2, z2_send, z2_recv)
                pivot[2, mine, :] = zgot2[z1]
                piv_start(2)

            @pl.when(core == 1)
            def _():
                a2a_wait(got23, got23_sem)

            panels_fill()
            p1_start()
            c1_wait()
            c2_start()

        @pl.when(b == 3)
        def _():
            @pl.when(core == 0)
            def _():
                piv_wait(2)
                sib_copy(2).start()

            @pl.when(core == 1)
            def _():
                sib_copy(1).wait_recv()
                sib_copy(2).wait_recv()

            p1_wait()
            p2_start()
            cross[...] = product(inverse[0], pivot[1], ROWS_COLS)
            work[1] = pivot[2] - product(cross[...], cross[...], COLS_COLS)

    def block_step(b, carry):
        comm(b)
        s = b // 3
        part = b % 3
        r0 = pl.multiple_of(part * TILE, TILE)
        tile = pl.ds(r0, TILE)
        rows = [
            work[s, pl.ds(pl.multiple_of(r0 + 8 * q, 8), 8), tile] for q in range(16)
        ]
        up, inv = factor_tile(rows)
        for q in range(16):
            at = pl.ds(pl.multiple_of(r0 + 8 * q, 8), 8)
            upper[s, at, tile] = up[q]
            inverse[s, at, tile] = inv[q]
        small = inverse[s, tile, tile]
        lanes = lax.broadcasted_iota(jnp.int32, (TILE, BLOCK), 1)
        after = lanes >= r0 + TILE
        before = lanes < r0
        down = jnp.where(after, product(small, work[s, tile, :], ROWS_COLS), 0.0)
        behind = jnp.where(before, product(small, ework[s, tile, :], ROWS_COLS), 0.0)
        upper[s, tile, :] += down
        inverse[s, tile, :] += behind

        @pl.when(part < 2)
        def _():
            work[s] -= product(down, down, COLS_COLS)
            ework[s] -= product(down, inverse[s, tile, :], COLS_COLS)

        return carry

    lax.fori_loop(0, 6, block_step, 0)

    j = col_order[col]
    mask0 = flag((pattern[j, 0] == 1) & (j > 0))
    mask1 = flag((pattern[j, 1] == 1) & (j > 1))
    is0, is1 = flag(j == 0), flag(j == 1)
    rest_of = flag(j > 1)
    v0 = split(inverse[0])
    v1 = split(inverse[1])
    cr = split(cross[...])

    place = [jnp.int32(0)] * 4
    for slot in range(4):
        for b in range(4):
            place[b] = place[b] + (order[slot] == b).astype(jnp.int32) * slot

    def scale(half, ref):
        for k in range(2):
            first = 1 - half
            i = row_order[row * 4 + first * order[k] + half * order[2 + k]]
            m0 = flag((pattern[i, 0] == 1) & (i > 0))
            m1 = flag((pattern[i, 1] == 1) & (i > 1))
            s0 = product3([(split(ref[0, k] * m0), v0)], ROWS_ROWS)
            rest = (ref[1, k] - product3([(split(s0), cr)], ROWS_COLS)) * m1
            scaled[half * 2 + k, 0] = s0
            scaled[half * 2 + k, 1] = product3([(split(rest), v1)], ROWS_ROWS)

    p2_wait()
    p3_copy().start()
    scale(core, panels_own)
    p3_copy().wait_recv()
    scale(1 - core, panels_sib)

    c2_wait()
    r0 = product3([(v0, split(turned[0] * mask0))], ROWS_COLS)
    r0s = split(r0)
    rest = (turned[1] - product3([(cr, r0s)], COLS_COLS)) * mask1
    r1s = split(product3([(v1, split(rest))], ROWS_COLS))

    factors = [upper[s].T * flag(j == s) for s in range(2)]
    for b in range(4):
        i = row_order[row * 4 + b]
        keep = flag((pattern[i, j] == 1) & (i >= j))
        center0, center1 = flag((i == 0) & (j == 0)), flag((i == 1) & (j == 1))
        s0, s1 = scaled[place[b], 0], scaled[place[b], 1]
        change = product3([(split(s0), r0s), (split(s1), r1s)], ROWS_COLS)
        value = (matrix[b] - change) * rest_of + s0 * is0 + s1 * is1
        out[b] = value * keep + factors[0] * center0 + factors[1] * center1
        pltpu.make_async_copy(out.at[b], out_hbm.at[b], store_sem.at[b]).start()

    for b in range(4):
        pltpu.make_async_copy(out.at[b], out_hbm.at[b], store_sem.at[b]).wait()
    a2a_sent(0)
    a2a_sent(1)
    a2a23_sent()
    p1_sent()
    p2_sent()
    p3_copy().wait_send()
    c1_sent()
    c2_sent()

    @pl.when(core == 0)
    def _():
        z_sent(zsend0, zgot0, z0_send, z0_recv)
        z_sent(zsend1, zgot1, z1_send, z1_recv)
        z_sent(zsend2, zgot2, z2_send, z2_recv)
        for block in range(3):
            piv_sent(block)
            sib_copy(block).wait_send()


def body(matrix, pattern, row_order, col_order):
    block = (BLOCK, BLOCK)
    vmem = lambda *shape: pltpu.VMEM(shape, F32)
    dma = lambda *shape: pltpu.SemaphoreType.DMA(shape)
    return pl.pallas_call(
        kernel,
        out_shape=jax.ShapeDtypeStruct((4, *block), F32),
        in_specs=[pl.BlockSpec(memory_space=pltpu.SMEM)] * 3
        + [pl.BlockSpec(memory_space=pl.ANY)],
        out_specs=pl.BlockSpec(memory_space=pl.ANY),
        scratch_shapes=[
            vmem(4, *block),
            vmem(4, *block),
            pltpu.SemaphoreType.DMA,
            dma(4),
            vmem(4, *block),
            vmem(*block),
            vmem(32, CHUNK, BLOCK),
            vmem(32, CHUNK, BLOCK),
            vmem(32, 2, CHUNK, BLOCK),
            vmem(CHUNK, BLOCK),
            vmem(CHUNK, BLOCK),
            vmem(CHUNK, BLOCK),
            vmem(8, CHUNK, BLOCK),
            vmem(8, CHUNK, BLOCK),
            vmem(8, CHUNK, BLOCK),
            vmem(3, *block),
            vmem(2, *block),
            vmem(2, *block),
            vmem(2, *block),
            vmem(2, *block),
            vmem(*block),
            vmem(2, 2, *block),
            vmem(2, 2, *block),
            vmem(2, 8, SHARE, BLOCK),
            vmem(2, *block),
            vmem(4, 2, *block),
            dma(3),
            pltpu.SemaphoreType.DMA,
            pltpu.SemaphoreType.DMA,
            pltpu.SemaphoreType.DMA,
            pltpu.SemaphoreType.DMA,
            pltpu.SemaphoreType.DMA,
            pltpu.SemaphoreType.DMA,
            pltpu.SemaphoreType.DMA,
            pltpu.SemaphoreType.DMA,
            pltpu.SemaphoreType.DMA,
            dma(3),
            dma(3),
            dma(3),
            dma(3),
            dma(2),
            dma(2),
            dma(2),
            dma(2),
            pltpu.SemaphoreType.DMA,
            pltpu.SemaphoreType.DMA,
            dma(2),
            dma(2),
            pltpu.SemaphoreType.DMA,
            pltpu.SemaphoreType.DMA,
        ],
        compiler_params=pltpu.CompilerParams(
            collective_id=0, has_side_effects=True, vmem_limit_bytes=60 * 2**20
        ),
    )(pattern, row_order, col_order, matrix.reshape(4, *block)).reshape(matrix.shape)


def solution(mesh):
    in_specs = (P("row", "col"), P(), P(), P())
    out_specs = P("row", "col")
    return jax.shard_map(body, mesh=mesh, in_specs=in_specs, out_specs=out_specs, check_vma=False)
```
